32 devices in a mesh: cells: 4 (over y, x), region: 8 (over z, core).
Axes of the slice: x: 2, y: 2, z: 4, core: 2. Of those that a mesh axis runs over, the one named last changes fastest.
Arguments:
- cell_shape: bfloat16 [32, 3, 544], P(('cells', 'region')), may hold values from -6 to 6
- upsample: bfloat16 [544, 2112], replicated, may hold values from -0.25 to 0.25
- bending: bfloat16 [544, 2112], replicated, may hold values from -0.25 to 0.25
- to_density: bfloat16 [2112, 152], replicated, may hold values from -0.125 to 0.125
- translate: bfloat16 [456, 456], replicated, may hold values from -0.25 to 0.25
- evaluate: bfloat16 [152, 2112], replicated, may hold values from -0.5 to 0.5
- smoothing: bfloat16 [2112, 544], replicated, may hold values from -0.125 to 0.125
- block_owner: int32 [8448, 1], P(('cells', 'region')), may hold values from 0 to 3; in each aligned block of 264 rows (0 to 263, 264 to 527, ...) at most 68 rows name the same one
- block_octant: int32 [8448], P(('cells', 'region')), may hold values from 0 to 7
- far_list: int32 [32, 8], P(('cells', 'region')), may hold values from 0 to 63
Outputs:
- velocity: float32 [32, 3, 544], P(('cells', 'region'))
The draws below stay inside these ranges and needn't reach their ends.
Inputs may be any that keep to these rules, and one draw needn't show every extreme that they name: `block_owner`: among the 264 blocks of one device no owner is named more than 68 times, and in some device's blocks one owner is named exactly 68 times.
All inputs are finite; a program needn't handle non-finite values.
Results may differ from the reference program's by a relative error of at most 0.0063.
Values may be sent and summed in bfloat16 or wider, within the bound.
No kernel may reach another device: no remote copies, remote signals or barrier semaphores. Data moves between devices by JAX's collectives and lax.ppermute only.
A program may use at most 64 MiB of HBM per device.

```python
import math
from functools import partial
import jax
import jax.numpy as jnp
import numpy as np
from jax import lax

P_COARSE = 544
P_FINE = 2112
EQ_PTS = 152
EQUIV = 456
BLK = 8
CELL_DEV = 1
NLIST = 8
OCT_DEV = 2
CELLS = 32
NB = 264
BLOCKS = 8448
OWNERS = 4
MOST = 68
OCT_R = 8
OCTANTS = 64
N_CELLS = 4
N_REGION = 8


def set_ends(drawn, stream_key, least, largest):
    place = [jax.random.randint(jax.random.fold_in(stream_key, axis), (), 0, length) for axis, length in enumerate(drawn.shape)]
    widest = drawn.shape.index(max(drawn.shape))
    neighbour = place[:widest] + [(place[widest] + 1) % drawn.shape[widest]] + place[widest + 1:]
    return drawn.at[tuple(place)].set(least).at[tuple(neighbour)].set(largest)


def block_levels(own_key, shape, pieces, low, top_value):
    gain = 1.0
    for axis_at, shards_of in pieces:
        steps = jax.random.uniform(jax.random.fold_in(jax.random.fold_in(own_key, 6), axis_at), (shards_of,), jnp.float32, low / len(pieces), top_value / len(pieces))
        gain = gain * jnp.repeat(jnp.exp(steps), shape[axis_at] // shards_of).reshape((-1,) + (1,) * (len(shape) - 1 - axis_at))
    return gain


def routed_block(own_key, own, number, rows, number_of, top, reach, lean):
    sequence = jax.random.permutation(own_key, number_of)
    heavy_load, common = portions_of(number_of, rows * top, reach, lean, True), portions_of(number_of, rows * top, reach, lean, False)
    places = jnp.arange(number_of)

    def named(sizes, rotation):
        used = int((sizes > 0).sum())
        fixed = max(1, used // 4)
        moved = fixed + (places - fixed + rotation * (used - fixed)) % max(1, number_of - fixed)
        return jnp.zeros((number_of,), jnp.int32).at[sequence[jnp.where(places < fixed, places, moved)]].set(jnp.asarray(sizes, jnp.int32))

    sizes = jnp.where(number % 4 == 0, named(heavy_load, number // 4), named(common, number - number // 4 - 1))
    mixed = jax.random.permutation(jax.random.fold_in(own, 3), number_of)
    source_of, receiver = mixed[0:number_of // 2 * 2:2], mixed[1:number_of // 2 * 2:2]
    margin = jnp.minimum(sizes[source_of] - 1, reach - sizes[receiver]) // 2
    margin = jnp.where((source_of == sequence[0]) | (receiver == sequence[0]) | (sizes[receiver] == 0), 0, jnp.maximum(margin, 0))
    moved = jax.random.randint(jax.random.fold_in(own, 4), (number_of // 2,), 0, 1 << 20) % (margin + 1)
    sizes = sizes.at[source_of].add(-moved).at[receiver].add(moved)
    labels = jnp.searchsorted(jnp.cumsum(sizes), jnp.arange(rows * top), side="right").astype(jnp.int32)
    table = labels.reshape(top, rows).T
    table = table[jax.random.permutation(jax.random.fold_in(own, 1), rows)]
    rotation = jax.random.randint(jax.random.fold_in(own, 2), (rows, 1), 0, top)
    return jnp.take_along_axis(table, (jnp.arange(top)[None, :] + rotation) % top, axis=1)


def portions_of(number_of, total, limit, skew, full):
    portions = [(1 << 20) // math.isqrt(standing ** skew) + 1 for standing in range(1, number_of + 1)]
    largest = limit if full else min(limit, max(-(-total // number_of), total * portions[0] // sum(portions)))
    least = 1 if total - largest >= number_of - 1 else 0
    given, rest = [largest] + [least] * (number_of - 1), total - largest - least * (number_of - 1)
    while rest > 0:
        movable = [i for i in range(1, number_of) if given[i] < largest] or [i for i in range(1, number_of) if given[i] < limit]
        pool, left = sum([portions[i] for i in movable]), rest
        for i in movable:
            more = min(limit - given[i], max(1, left * portions[i] // pool), rest)
            given[i] = given[i] + more
            rest = rest - more
    return np.array(given)


def noise(rng, extent, deviation, most, pieces=(), kind=jnp.bfloat16):
    factor_of = block_levels(rng, extent, pieces, -0.22, 0.18) if pieces else 1.0
    entries = jax.random.normal(rng, extent, jnp.float32) * deviation * factor_of
    return jnp.minimum(jnp.maximum(entries, -most), most).astype(kind)


def setup_inputs(seed: int = 0) -> dict:
    splits = jax.random.split(jax.random.key(seed), 11)
    cell_shape = noise(splits[0], (CELLS, 3, P_COARSE), 1.0, 6.0, ((0, 32),))
    upsample = noise(splits[1], (P_COARSE, P_FINE), P_COARSE ** -0.5, 0.25)
    bending = noise(splits[2], (P_COARSE, P_FINE), P_COARSE ** -0.5, 0.25)
    to_density = noise(splits[3], (P_FINE, EQ_PTS), P_FINE ** -0.5, 0.125)
    translate = noise(splits[4], (EQUIV, EQUIV), EQUIV ** -0.5, 0.25)
    evaluate = noise(splits[5], (EQ_PTS, P_FINE), EQ_PTS ** -0.5, 0.5)
    smoothing = noise(splits[6], (P_FINE, P_COARSE), P_FINE ** -0.5, 0.125)
    block_owner_keys = jax.random.split(jax.random.fold_in(splits[7], 1), BLOCKS // NB)
    block_owner_turns = jax.random.permutation(jax.random.fold_in(splits[7], 3), BLOCKS // NB)
    block_owner = jax.vmap(lambda own, number: routed_block(jax.random.fold_in(splits[7], 2), own, number, NB, OWNERS, 1, MOST, 2))(block_owner_keys, block_owner_turns).reshape((BLOCKS, 1))
    block_octant = set_ends(jax.random.randint(splits[8], (BLOCKS,), 0, OCT_R), jax.random.fold_in(splits[8], 1), 0, OCT_R - 1).astype(jnp.int32)
    far_list = set_ends(jax.random.randint(splits[9], (CELLS, NLIST), 0, OCTANTS), jax.random.fold_in(splits[9], 1), 0, OCTANTS - 1).astype(jnp.int32)
    return {"cell_shape": cell_shape, "upsample": upsample, "bending": bending, "to_density": to_density, "translate": translate, "evaluate": evaluate, "smoothing": smoothing, "block_owner": block_owner, "block_octant": block_octant, "far_list": far_list}


EPSILON_SQ = 0.0625
STOKES_SCALE = 1.0 / (8.0 * 3.141592653589793)

def stokeslet(targets, sources, strength):
    diff_x = targets[0][:, None] - sources[0][None, :]
    diff_y = targets[1][:, None] - sources[1][None, :]
    diff_z = targets[2][:, None] - sources[2][None, :]
    radius_sq = diff_x * diff_x + diff_y * diff_y + diff_z * diff_z + EPSILON_SQ
    inverse = lax.rsqrt(radius_sq)
    cubed = inverse * inverse * inverse
    direct = (radius_sq + EPSILON_SQ) * cubed
    radial = (diff_x * strength[0][None, :] + diff_y * strength[1][None, :] + diff_z * strength[2][None, :]) * cubed
    vel_x = lax.optimization_barrier(jnp.sum(direct * strength[0][None, :] + diff_x * radial, axis=1))
    vel_y = lax.optimization_barrier(jnp.sum(direct * strength[1][None, :] + diff_y * radial, axis=1))
    vel_z = lax.optimization_barrier(jnp.sum(direct * strength[2][None, :] + diff_z * radial, axis=1))
    return jnp.stack([vel_x, vel_y, vel_z]) * STOKES_SCALE

def near_field(leaf_points):
    sources = leaf_points[:3].astype(jnp.float32)
    strength = leaf_points[3:].astype(jnp.float32)
    point_total = sources.shape[1]
    padding = -point_total % 256
    padded = jnp.pad(sources, ((0, 0), (0, padding)))
    tile_set = padded.reshape(3, -1, 256).transpose(1, 0, 2)
    result = lax.map(partial(stokeslet, sources=sources, strength=strength), tile_set)
    return result.transpose(1, 0, 2).reshape(3, -1)[:, :point_total]

def slot_numbers(owner, owners_count, capacity):
    onehot = (owner[:, None] == jnp.arange(owners_count, dtype=jnp.int32)[None, :]).astype(jnp.int32)
    before = jnp.cumsum(onehot, axis=0) - onehot
    slot_rank = lax.optimization_barrier(jnp.sum(before * onehot, axis=1))
    return (owner * capacity + slot_rank).astype(jnp.int32)

def place_blocks(block_data, slot_index, slot_total):
    empty = jnp.zeros((slot_total,) + block_data.shape[1:], block_data.dtype)
    return empty.at[slot_index].set(block_data)

def pick_blocks(returned, slot_index):
    return returned[slot_index]

def region_density(inputs_pair, to_density):
    region_forces, region_octant = inputs_pair
    octant_rows = OCT_DEV * N_CELLS
    choose = region_octant[None] == jnp.arange(octant_rows, dtype=jnp.int32)[:, None, None]
    masked = jnp.where(choose[:, :, None, :], region_forces[None], jnp.zeros((), region_forces.dtype))
    product = jnp.dot(masked.reshape(-1, P_FINE), to_density, preferred_element_type=jnp.float32)
    product = product.reshape(octant_rows, -1, 3 * EQ_PTS)
    return lax.optimization_barrier(jnp.sum(product, axis=1))

def reference(cell_shape, upsample, bending, to_density, translate, evaluate, smoothing, block_owner, block_octant, far_list):
    devices = N_CELLS * N_REGION
    per_cell = P_FINE // BLK
    block_count = CELL_DEV * per_cell
    capacity = block_count // N_CELLS + 2
    coarse = cell_shape.reshape(CELLS * 3, P_COARSE)
    points = jnp.dot(coarse, upsample, preferred_element_type=jnp.float32).astype(jnp.bfloat16).reshape(CELLS, 3, P_FINE)
    forces = jnp.dot(coarse, bending, preferred_element_type=jnp.float32).astype(jnp.bfloat16).reshape(CELLS, 3, P_FINE)
    stacked = jnp.concatenate([points, forces], axis=1)
    blocks = stacked.reshape(devices, CELL_DEV, 6, per_cell, BLK).transpose(0, 1, 3, 2, 4).reshape(devices, block_count, 6, BLK)
    owners = block_owner.reshape(devices, block_count)
    slot_index = jax.vmap(partial(slot_numbers, owners_count=N_CELLS, capacity=capacity))(owners)
    buffers = jax.vmap(partial(place_blocks, slot_total=N_CELLS * capacity))(blocks, slot_index)
    buffers = buffers.reshape(N_CELLS, N_REGION, N_CELLS, capacity, 6, BLK)
    leaves = buffers.transpose(1, 2, 4, 0, 3, 5).reshape(N_REGION * N_CELLS, 6, N_CELLS * capacity * BLK)
    near_vel = lax.map(near_field, leaves)
    near_vel = near_vel.reshape(N_REGION, N_CELLS, 3, N_CELLS, capacity, BLK).transpose(3, 0, 1, 4, 2, 5)
    near_vel = near_vel.reshape(devices, N_CELLS * capacity, 3, BLK)
    own_blocks = jax.vmap(pick_blocks)(near_vel, slot_index)
    near_points = own_blocks.reshape(devices, CELL_DEV, per_cell, 3, BLK).transpose(0, 1, 3, 2, 4).reshape(CELLS, 3, P_FINE)
    octant_blocks = block_octant.reshape(devices, CELL_DEV, per_cell, 1)
    point_octant = jnp.broadcast_to(octant_blocks, (devices, CELL_DEV, per_cell, BLK)).reshape(N_CELLS, N_REGION, CELL_DEV, P_FINE)
    region_forces = forces.reshape(N_CELLS, N_REGION, CELL_DEV, 3, P_FINE).transpose(1, 0, 2, 3, 4).reshape(N_REGION, N_CELLS * CELL_DEV, 3, P_FINE)
    region_octant = point_octant.transpose(1, 0, 2, 3).reshape(N_REGION, N_CELLS * CELL_DEV, P_FINE)
    density = lax.map(partial(region_density, to_density=to_density), (region_forces, region_octant))
    density_round = density.astype(jnp.bfloat16).reshape(-1, 3 * EQ_PTS)
    expansion = jnp.dot(density_round, translate, preferred_element_type=jnp.float32).astype(jnp.bfloat16)
    far_sum = lax.optimization_barrier(jnp.sum(expansion[far_list].astype(jnp.float32), axis=1))
    far_round = far_sum.astype(jnp.bfloat16).reshape(CELLS * 3, EQ_PTS)
    far_velocity = jnp.dot(far_round, evaluate, preferred_element_type=jnp.float32).reshape(CELLS, 3, P_FINE)
    total = (near_points + far_velocity).astype(jnp.bfloat16)
    velocity = jnp.dot(total.reshape(CELLS * 3, P_FINE), smoothing, preferred_element_type=jnp.float32)
    return velocity.reshape(CELLS, 3, P_COARSE)
```

```python
import functools

import jax
import jax.numpy as jnp
from jax import lax
from jax.experimental import pallas as pl
from jax.experimental.pallas import tpu as pltpu
from jax.sharding import PartitionSpec as P

EPSILON_SQ = 0.0625
STOKES_SCALE = 1.0 / (8.0 * 3.141592653589793)
EXPAND_LIMIT = 256.0
TILE = 256
OCTANTS_PER_OWNER = 2
F32 = jnp.float32
BF16 = jnp.bfloat16
LANES = (((1,), (1,)), ((), ()))


def iota(shape, dim):
    return lax.broadcasted_iota(jnp.int32, shape, dim)


def dot(a, b):
    return jnp.dot(a, b, preferred_element_type=F32)


def dot_lanes(a, b):
    return lax.dot_general(a, b, LANES, preferred_element_type=F32)


def split_bf16(x):
    high = x.astype(BF16)
    return high, (x - high.astype(F32)).astype(BF16)


def pack_kernel(cell_ref, owner_ref, octant_ref, pack_ref, spread_ref):
    nb = owner_ref.shape[1]
    width = cell_ref.shape[1]
    pack_ref[0:3, :] = cell_ref[...]
    row = jnp.concatenate(
        [
            owner_ref[...].astype(F32),
            octant_ref[...].astype(F32),
            jnp.zeros((1, width - 2 * nb), F32),
        ],
        axis=1,
    )
    pack_ref[3:4, :] = row.astype(BF16)
    spread_ref[...] = jnp.broadcast_to(pack_ref[...][None], spread_ref.shape)


def interleave_matrix(blk):
    group = TILE // blk
    point, lane = iota((TILE, TILE), 0), iota((TILE, TILE), 1)
    return ((point % blk == lane // group) & (point // blk == lane % group)).astype(BF16)


def source_columns(rows):
    forces = jnp.concatenate([rows[4:8], rows[4:8]], axis=0)
    places = jnp.concatenate([rows[0:4], rows[0:4]], axis=0)
    upper = iota(rows.shape, 0) < 4
    groups = []
    square = jnp.zeros_like(rows)
    inner = jnp.zeros_like(rows)
    for k in range(3):
        x_k = jnp.broadcast_to(rows[k : k + 1], rows.shape)
        product = x_k * forces
        high = product.astype(BF16).astype(F32)
        groups.append(jnp.where(upper, high, product - high))
        square = square + x_k * x_k
        inner = inner + x_k * rows[4 + k : 5 + k]
    rest = square * forces + inner * places
    high = rest.astype(BF16).astype(F32)
    middle = (rest - high).astype(BF16).astype(F32)
    groups.append(jnp.where(upper, high, middle))
    groups.append(jnp.where(upper, rest - high - middle, forces))
    return jnp.concatenate(groups, axis=0).astype(BF16)


def squared_distance(spread, rows, start, stop):
    total = None
    diffs = []
    for k in range(3):
        diff = jnp.concatenate([spread[k]] * ((stop - start) // 128), axis=1) - rows[k : k + 1, start:stop]
        diffs.append(diff)
        term = diff * diff
        total = term + EPSILON_SQ if total is None else total + term
    return total, diffs


def expanded_sums(spread, rows, targets):
    columns = source_columns(rows)
    sums = None
    for start in range(0, rows.shape[1], TILE):
        stop = min(start + TILE, rows.shape[1])
        dist, _ = squared_distance(spread, rows, start, stop)
        inverse = lax.rsqrt(dist)
        cubed = (inverse * inverse * inverse).astype(BF16)
        part = dot_lanes(columns[:, start:stop], cubed)
        sums = part if sums is None else sums + part
    place = targets[0:4]
    moment = [sums[8 * k : 8 * k + 4] + sums[8 * k + 4 : 8 * k + 8] for k in range(3)]
    rest = sums[24:28] + sums[28:32] + sums[32:36]
    force = sums[36:40]
    square = jnp.sum(place * place, axis=0, keepdims=True)
    along = jnp.sum(place * force, axis=0, keepdims=True)
    trace = moment[0][0:1] + moment[1][1:2] + moment[2][2:3]
    cross = [jnp.sum(place * moment[k], axis=0, keepdims=True) for k in range(3)]
    cross = jnp.concatenate(cross + [jnp.zeros_like(trace)], axis=0)
    weighted = place[0:1] * moment[0] + place[1:2] * moment[1] + place[2:3] * moment[2]
    return (
        (square + 2.0 * EPSILON_SQ) * force + rest - 2.0 * weighted + place * (along - trace) - cross
    )


def direct_sums(spread, rows, targets):
    strength = rows[4:8].astype(BF16)
    ones = jnp.ones((1, rows.shape[1]), F32)
    places = jnp.concatenate([rows[0:3], ones], axis=0).astype(BF16)
    sums = None
    for start in range(0, rows.shape[1], TILE):
        stop = min(start + TILE, rows.shape[1])
        dist, diffs = squared_distance(spread, rows, start, stop)
        inverse = lax.rsqrt(dist)
        cubed = inverse * inverse * inverse
        direct = ((dist + EPSILON_SQ) * cubed).astype(BF16)
        along = sum(diffs[k] * rows[4 + k : 5 + k, start:stop] for k in range(3))
        radial = (along * cubed).astype(BF16)
        near = dot_lanes(strength[:, start:stop], direct)
        away = dot_lanes(places[:, start:stop], radial)
        part = jnp.concatenate([near, away], axis=0)
        sums = part if sums is None else sums + part
    return sums[0:4] + targets[0:4] * sums[7:8] - sums[4:8]


def near_kernel(blk, *refs):
    *pack_refs, up_ref, bend_ref, out_ref = refs
    packs = []
    for ref in pack_refs:
        if len(ref.shape) == 2:
            packs.append(ref[...])
        else:
            packs += [ref[i] for i in range(ref.shape[0])]
    cells = len(packs)
    fine = up_ref.shape[1]
    nb = fine // blk
    capacity = nb // cells + 2
    spots = cells * capacity
    group = TILE // blk
    tiles = -(-fine // TILE)
    point_rows, force_rows, owners = [], [], []
    for pack in packs:
        pack = pack.astype(F32)
        owners.append(pack[3:4, 0:nb])
        three = jnp.where(iota((4, pack.shape[1]), 0) < 3, pack[0:4], 0.0)
        point_rows += [three, jnp.zeros_like(three)]
        force_rows += [jnp.zeros_like(three), three]
    point_rows = jnp.concatenate(point_rows, axis=0).astype(BF16)
    force_rows = jnp.concatenate(force_rows, axis=0).astype(BF16)
    fields = (dot(point_rows, up_ref[...]) + dot(force_rows, bend_ref[...])).astype(BF16)
    fields = jnp.concatenate(
        [fields, jnp.zeros((8 * cells, tiles * TILE - fine), BF16)], axis=1
    )
    mix = interleave_matrix(blk)
    stacked = jnp.concatenate(
        [fields[:, t * TILE : (t + 1) * TILE] for t in range(tiles)], axis=0
    )
    parted = dot(stacked, mix)
    by_point = [
        jnp.concatenate(
            [
                parted[t * 8 * cells : (t + 1) * 8 * cells, k * group : (k + 1) * group]
                for t in range(tiles)
            ],
            axis=1,
        )[:, 0:nb]
        for k in range(blk)
    ]
    leaf_ids = iota((cells, nb), 0).astype(F32)
    chosen = jnp.concatenate([(leaf_ids == own).astype(F32) for own in owners], axis=0)
    earlier = (iota((nb, nb), 0) < iota((nb, nb), 1)).astype(BF16)
    before = dot(chosen.astype(BF16), earlier) * chosen
    spot_ids = iota((spots, nb), 0).astype(F32)
    sorts, by_leaf = [], []
    for c in range(cells):
        rank = jnp.sum(before[c * cells : (c + 1) * cells], axis=0, keepdims=True)
        sorts.append((spot_ids == owners[c] * capacity + rank).astype(BF16))
        rows = jnp.concatenate([by_point[k][8 * c : 8 * c + 8] for k in range(blk)], axis=0)
        by_leaf.append(dot_lanes(rows.astype(BF16), sorts[c]))
    farthest = jnp.max(
        sum(jnp.square(by_leaf[c][8 * k : 8 * k + 4]) for c in range(cells) for k in range(blk))
    )

    def all_leaves(sums):
        found = []
        for leaf in range(cells):
            rows = jnp.concatenate(
                [
                    by_leaf[c][8 * k : 8 * k + 8, leaf * capacity : (leaf + 1) * capacity]
                    for c in range(cells)
                    for k in range(blk)
                ],
                axis=1,
            )
            targets = rows[:, 0 : capacity * blk]
            upright = targets.T
            spread = [
                jnp.broadcast_to(upright[:, k : k + 1], (capacity * blk, 128)) for k in range(3)
            ]
            velocity = sums(spread, rows, targets) * STOKES_SCALE
            found.append(
                jnp.concatenate(
                    [velocity[:, k * capacity : (k + 1) * capacity] for k in range(blk)], axis=0
                )
            )
        found = jnp.concatenate(found, axis=1)
        high, low = split_bf16(found)
        back = dot(jnp.concatenate([high, low], axis=0), sorts[0])
        back = back[: 4 * blk] + back[4 * blk :]
        back = jnp.concatenate(
            [back, jnp.zeros((4 * blk, tiles * group - nb), F32)], axis=1
        )
        pieces = [
            jnp.concatenate(
                [back[4 * k : 4 * k + 4, t * group : (t + 1) * group] for k in range(blk)], axis=1
            )
            for t in range(tiles)
        ]
        high, low = split_bf16(jnp.concatenate(pieces, axis=0))
        natural = dot_lanes(high, mix) + dot_lanes(low, mix)
        for t in range(tiles):
            stop = min((t + 1) * TILE, fine)
            out_ref[0:4, t * TILE : stop] = natural[4 * t : 4 * t + 4, 0 : stop - t * TILE]

    small = farthest <= EXPAND_LIMIT
    pl.when(small)(functools.partial(all_leaves, expanded_sums))
    pl.when(jnp.logical_not(small))(functools.partial(all_leaves, direct_sums))


def far_kernel(blk, cells, regions, list_ref, packs_ref, near_ref, bend_ref, dens_ref, trans_ref, eval_ref, smooth_ref, out_ref):
    listed = list_ref.shape[1]
    fine = bend_ref.shape[1]
    nb = fine // blk
    points = eval_ref.shape[0]
    per_region = OCTANTS_PER_OWNER * cells
    rows = cells * 3 * listed
    devices = cells * regions
    row = iota((rows, 1), 0)
    entry, comp, cell = row % listed, row // listed % 3, row // (3 * listed)
    octant = jnp.zeros((rows, 1), jnp.int32)
    region = jnp.zeros((rows, 1), jnp.int32)
    for l in range(listed):
        wanted = list_ref[0, l]
        octant = jnp.where(entry == l, wanted % per_region, octant)
        region = jnp.where(entry == l, wanted // per_region, region)
    source = (cell * regions + region) * 4
    columns = iota((rows, devices * 4), 1)
    flat = packs_ref[...].reshape(devices * 4, packs_ref.shape[2])
    coarse = dot((columns == source + comp).astype(BF16), flat)
    marks = dot((columns == source + 3).astype(BF16), flat)
    inside = (marks[:, nb : 2 * nb] == octant.astype(F32)).astype(BF16)
    widen = (iota((nb, fine), 0) == iota((nb, fine), 1) // blk).astype(BF16)
    inside = dot(inside, widen)
    forces = dot(coarse.astype(BF16), bend_ref[...]).astype(BF16).astype(F32)
    density = dot_lanes((forces * inside).astype(BF16), dens_ref[...])
    span = 3 * listed
    density = sum(density[c * span : (c + 1) * span] for c in range(cells)).astype(BF16)
    expansion = sum(
        dot(density[k * listed : (k + 1) * listed], trans_ref[k * points : (k + 1) * points, :])
        for k in range(3)
    )
    far = jnp.sum(expansion.astype(BF16).astype(F32), axis=0, keepdims=True)
    far = jnp.concatenate(
        [far[:, k * points : (k + 1) * points] for k in range(3)] + [jnp.zeros((1, points), F32)],
        axis=0,
    )
    total = near_ref[0:4, :] + dot(far.astype(BF16), eval_ref[...])
    velocity = dot_lanes(total.astype(BF16), smooth_ref[...])
    for k in range(3):
        out_ref[k] = velocity[k : k + 1]


def vmem(megabytes):
    return pltpu.CompilerParams(vmem_limit_bytes=megabytes << 20)


def on_device(
    cell_shape,
    upsample,
    bending,
    to_density,
    translate,
    evaluate,
    smoothing,
    block_owner,
    block_octant,
    far_list,
):
    cells, regions = lax.axis_size("cells"), lax.axis_size("region")
    coarse, fine = upsample.shape
    nb = block_owner.shape[0]
    blk = fine // nb
    pack, spread = pl.pallas_call(
        pack_kernel,
        out_shape=(
            jax.ShapeDtypeStruct((4, coarse), BF16),
            jax.ShapeDtypeStruct((cells * regions, 4, coarse), BF16),
        ),
        name="pack",
    )(cell_shape.reshape(3, coarse), block_owner.reshape(1, nb), block_octant.reshape(1, nb))
    others = [
        lax.ppermute(pack, "cells", [(i, i ^ k) for i in range(cells)])
        for k in sorted(range(1, cells), reverse=True)
    ]
    everyone = lax.all_to_all(spread, ("cells", "region"), split_axis=0, concat_axis=0, tiled=True)
    near = pl.pallas_call(
        functools.partial(near_kernel, blk),
        out_shape=jax.ShapeDtypeStruct((4, fine), F32),
        compiler_params=vmem(32),
        cost_estimate=pl.CostEstimate(flops=5 * 10**9, bytes_accessed=10**6, transcendentals=0),
        name="near",
    )(pack, *others, upsample, bending)
    in_vmem = pl.BlockSpec(memory_space=pltpu.VMEM)
    velocity = pl.pallas_call(
        functools.partial(far_kernel, blk, cells, regions),
        out_shape=jax.ShapeDtypeStruct((3, 1, coarse), F32),
        in_specs=[pl.BlockSpec(memory_space=pltpu.SMEM)] + [in_vmem] * 7,
        compiler_params=vmem(32),
        name="far",
    )(far_list, everyone, near, bending, to_density.T, translate, evaluate, smoothing.T)
    return velocity.transpose(1, 0, 2)


def solution(mesh):
    own = P(("cells", "region"))
    return jax.shard_map(
        on_device,
        mesh=mesh,
        in_specs=(own, P(), P(), P(), P(), P(), P(), own, own, own),
        out_specs=own,
        check_vma=False,
    )
```

```python
import functools

import jax
import jax.numpy as jnp
from jax import lax
from jax.experimental import pallas as pl
from jax.experimental.pallas import tpu as pltpu
from jax.sharding import PartitionSpec as P

EPSILON_SQ = 0.0625
STOKES_SCALE = 1.0 / (8.0 * 3.141592653589793)
EXPAND_LIMIT = 128.0
TILE = 256
OCTANTS_PER_OWNER = 2
F32 = jnp.float32
BF16 = jnp.bfloat16
LANES = (((1,), (1,)), ((), ()))


def iota(shape, dim):
    return lax.broadcasted_iota(jnp.int32, shape, dim)


def dot(a, b):
    return jnp.dot(a, b, preferred_element_type=F32)


def dot_lanes(a, b):
    return lax.dot_general(a, b, LANES, preferred_element_type=F32)


def split_bf16(x):
    high = x.astype(BF16)
    return high, (x - high.astype(F32)).astype(BF16)


def row_chunks(rows):
    return [(start, min(start + TILE, rows)) for start in range(0, rows, TILE)]


class Arriving:
    def __init__(self, sources, targets, sems):
        self.targets = targets
        self.pieces = [
            [
                (pltpu.make_async_copy(src.at[a:b], dst.at[a:b], sems.at[n, i]), a, b)
                for i, (a, b) in enumerate(row_chunks(src.shape[0]))
            ]
            for n, (src, dst) in enumerate(zip(sources, targets))
        ]

    def start(self, n):
        for copy, _, _ in self.pieces[n]:
            copy.start()

    def wait(self, n):
        for copy, _, _ in self.pieces[n]:
            copy.wait()

    def dot(self, lhs, n):
        total = None
        for copy, a, b in self.pieces[n]:
            copy.wait()
            part = dot(lhs[:, a:b], self.targets[n][a:b, :])
            total = part if total is None else total + part
        return total


def pack_kernel(cell_ref, owner_ref, octant_ref, pack_ref, spread_ref):
    nb = owner_ref.shape[1]
    width = cell_ref.shape[1]
    octant = octant_ref[...].reshape(1, nb)
    pack_ref[0:3, :] = cell_ref[...]
    row = jnp.concatenate(
        [
            owner_ref[...].astype(F32),
            octant.astype(F32),
            jnp.zeros((1, width - 2 * nb), F32),
        ],
        axis=1,
    )
    pack_ref[3:4, :] = row.astype(BF16)
    spread_ref[...] = jnp.broadcast_to(pack_ref[...][None], spread_ref.shape)


def interleave_matrix(blk):
    group = TILE // blk
    point, lane = iota((TILE, TILE), 0), iota((TILE, TILE), 1)
    return ((point % blk == lane // group) & (point // blk == lane % group)).astype(BF16)


def source_columns(rows):
    forces = jnp.concatenate([rows[4:8], rows[4:8]], axis=0)
    places = jnp.concatenate([rows[0:4], rows[0:4]], axis=0)
    upper = iota(rows.shape, 0) < 4
    groups = []
    square = jnp.zeros_like(rows)
    inner = jnp.zeros_like(rows)
    for k in range(3):
        x_k = jnp.broadcast_to(rows[k : k + 1], rows.shape)
        product = x_k * forces
        high = product.astype(BF16).astype(F32)
        groups.append(jnp.where(upper, high, product - high))
        square = square + x_k * x_k
        inner = inner + x_k * rows[4 + k : 5 + k]
    rest = square * forces + inner * places
    high = rest.astype(BF16).astype(F32)
    middle = (rest - high).astype(BF16).astype(F32)
    groups.append(jnp.where(upper, high, middle))
    groups.append(jnp.where(upper, rest - high - middle, forces))
    return jnp.concatenate(groups, axis=0).astype(BF16)


def three_parts(x):
    high = x.astype(BF16).astype(F32)
    middle = (x - high).astype(BF16).astype(F32)
    return high, middle, x - high - middle


def distance_factors(rows, targets):
    def side(points, scale, extra, squares_first):
        square = jnp.sum(jnp.square(points[0:4]), axis=0, keepdims=True) + extra
        ones = [jnp.ones_like(square)] * 3
        squares = list(three_parts(square))
        parts = squares + ones if squares_first else ones + squares
        unused = jnp.zeros((7, points.shape[1]), F32)
        return jnp.concatenate([points[0:3] * scale] + parts + [unused], axis=0)

    source = side(rows, -2.0, 0.0, False).astype(BF16)
    target = side(targets, 1.0, EPSILON_SQ, True).T.astype(BF16)
    return source, target


def expanded_sums(rows, targets):
    columns = source_columns(rows)
    source, target = distance_factors(rows, targets)
    inverse = lax.rsqrt(dot(target, source))
    cubed = (inverse * inverse * inverse).astype(BF16)
    sums = dot_lanes(columns, cubed)
    place = targets[0:4]
    moment = [sums[8 * k : 8 * k + 4] + sums[8 * k + 4 : 8 * k + 8] for k in range(3)]
    rest = sums[24:28] + sums[28:32] + sums[32:36]
    force = sums[36:40]
    square = jnp.sum(place * place, axis=0, keepdims=True)
    along = jnp.sum(place * force, axis=0, keepdims=True)
    trace = moment[0][0:1] + moment[1][1:2] + moment[2][2:3]
    cross = [jnp.sum(place * moment[k], axis=0, keepdims=True) for k in range(3)]
    cross = jnp.concatenate(cross + [jnp.zeros_like(trace)], axis=0)
    weighted = place[0:1] * moment[0] + place[1:2] * moment[1] + place[2:3] * moment[2]
    return (
        (square + 2.0 * EPSILON_SQ) * force + rest - 2.0 * weighted + place * (along - trace) - cross
    )


def direct_sums(rows, targets):
    strength = rows[4:8].astype(BF16)
    ones = jnp.ones((1, rows.shape[1]), F32)
    places = jnp.concatenate([rows[0:3], ones], axis=0).astype(BF16)
    upright = targets.T
    sums = None
    for start in range(0, rows.shape[1], TILE):
        stop = min(start + TILE, rows.shape[1])
        diffs = [upright[:, k : k + 1] - rows[k : k + 1, start:stop] for k in range(3)]
        dist = diffs[0] * diffs[0] + diffs[1] * diffs[1] + diffs[2] * diffs[2] + EPSILON_SQ
        inverse = lax.rsqrt(dist)
        cubed = inverse * inverse * inverse
        direct = ((dist + EPSILON_SQ) * cubed).astype(BF16)
        along = sum(diffs[k] * rows[4 + k : 5 + k, start:stop] for k in range(3))
        radial = (along * cubed).astype(BF16)
        near = dot_lanes(strength[:, start:stop], direct)
        away = dot_lanes(places[:, start:stop], radial)
        part = jnp.concatenate([near, away], axis=0)
        sums = part if sums is None else sums + part
    return sums[0:4] + targets[0:4] * sums[7:8] - sums[4:8]


def near_kernel(blk, packs_given, *refs):
    cell_ref, owner_ref, *pack_refs = refs[: packs_given + 2]
    bend_ref, up_hbm, out_ref, up_ref, rows_ref, found_ref, sems = refs[packs_given + 2 :]
    arriving = Arriving([up_hbm], [up_ref], sems)
    arriving.start(0)
    packs = [ref[...].astype(F32) for ref in pack_refs]
    cells = len(packs) + 1
    fine = up_ref.shape[1]
    nb = fine // blk
    capacity = nb // cells + 2
    spots = cells * capacity
    group = TILE // blk
    tiles = -(-fine // TILE)
    point_rows, force_rows = [], []
    coarse = [jnp.concatenate([cell_ref[...].astype(F32), jnp.zeros((1, cell_ref.shape[1]), F32)], axis=0)]
    coarse += [jnp.where(iota(pack.shape, 0) < 3, pack, 0.0) for pack in packs]
    owners = [owner_ref[...].astype(F32)] + [pack[3:4, 0:nb] for pack in packs]
    for three in coarse:
        point_rows += [three, jnp.zeros_like(three)]
        force_rows += [jnp.zeros_like(three), three]
    point_rows = jnp.concatenate(point_rows, axis=0).astype(BF16)
    force_rows = jnp.concatenate(force_rows, axis=0).astype(BF16)
    leaf_ids = iota((cells, nb), 0).astype(F32)
    chosen = jnp.concatenate([(leaf_ids == own).astype(F32) for own in owners], axis=0)
    earlier = (iota((nb, nb), 0) < iota((nb, nb), 1)).astype(BF16)
    before = dot(chosen.astype(BF16), earlier) * chosen
    spot_ids = iota((spots, nb), 0).astype(F32)
    sorts = []
    for c in range(cells):
        rank = jnp.sum(before[c * cells : (c + 1) * cells], axis=0, keepdims=True)
        sorts.append((spot_ids == owners[c] * capacity + rank).astype(BF16))
    mix = interleave_matrix(blk)
    fields = (dot(force_rows, bend_ref[...]) + arriving.dot(point_rows, 0)).astype(BF16)
    fields = jnp.concatenate(
        [fields, jnp.zeros((8 * cells, tiles * TILE - fine), BF16)], axis=1
    )
    stacked = jnp.concatenate(
        [fields[:, t * TILE : (t + 1) * TILE] for t in range(tiles)], axis=0
    )
    parted = dot(stacked, mix)
    by_point = [
        jnp.concatenate(
            [
                parted[t * 8 * cells : (t + 1) * 8 * cells, k * group : (k + 1) * group]
                for t in range(tiles)
            ],
            axis=1,
        )[:, 0:nb]
        for k in range(blk)
    ]
    by_leaf = []
    for c in range(cells):
        rows = jnp.concatenate([by_point[k][8 * c : 8 * c + 8] for k in range(blk)], axis=0)
        by_leaf.append(dot_lanes(rows.astype(BF16), sorts[c]))
    for leaf in range(cells):
        rows_ref[leaf] = jnp.concatenate(
            [
                by_leaf[c][8 * k : 8 * k + 8, leaf * capacity : (leaf + 1) * capacity]
                for c in range(cells)
                for k in range(blk)
            ],
            axis=1,
        )
    farthest = jnp.max(
        sum(jnp.square(by_leaf[c][8 * k : 8 * k + 4]) for c in range(cells) for k in range(blk))
    )

    def each_leaf(sums, leaf, _):
        rows = rows_ref[leaf]
        velocity = sums(rows, rows[:, 0 : capacity * blk]) * STOKES_SCALE
        found_ref[leaf] = jnp.concatenate(
            [velocity[:, k * capacity : (k + 1) * capacity] for k in range(blk)], axis=0
        )
        return 0

    lax.fori_loop(0, cells, functools.partial(each_leaf, expanded_sums), 0, unroll=cells <= 4)

    @pl.when(farthest > EXPAND_LIMIT)
    def _():
        lax.fori_loop(0, cells, functools.partial(each_leaf, direct_sums), 0)

    found = jnp.concatenate([found_ref[leaf] for leaf in range(cells)], axis=1)
    high, low = split_bf16(found)
    back = dot(jnp.concatenate([high, low], axis=0), sorts[0])
    back = back[: 4 * blk] + back[4 * blk :]
    back = jnp.concatenate([back, jnp.zeros((4 * blk, tiles * group - nb), F32)], axis=1)
    pieces = [
        jnp.concatenate(
            [back[4 * k : 4 * k + 4, t * group : (t + 1) * group] for k in range(blk)], axis=1
        )
        for t in range(tiles)
    ]
    high, low = split_bf16(jnp.concatenate(pieces, axis=0))
    natural = dot_lanes(high, mix) + dot_lanes(low, mix)
    for t in range(tiles):
        stop = min((t + 1) * TILE, fine)
        out_ref[0:4, t * TILE : stop] = natural[4 * t : 4 * t + 4, 0 : stop - t * TILE]

def far_kernel(blk, cells, regions, *refs):
    list_ref, packs_ref, near_ref, bend_ref, *in_hbm = refs[:8]
    out_ref, *in_vmem, sems = refs[8:]
    dens_ref, trans_ref, eval_ref, smooth_ref = in_vmem
    arriving = Arriving(in_hbm, in_vmem, sems)
    for n in range(len(in_hbm)):
        arriving.start(n)
    listed = list_ref.shape[1]
    fine = bend_ref.shape[1]
    nb = fine // blk
    points = eval_ref.shape[0]
    per_region = OCTANTS_PER_OWNER * cells
    rows = cells * 3 * listed
    devices = cells * regions
    row = iota((rows, 1), 0)
    entry, comp, cell = row % listed, row // listed % 3, row // (3 * listed)
    octant = jnp.zeros((rows, 1), jnp.int32)
    region = jnp.zeros((rows, 1), jnp.int32)
    for l in range(listed):
        wanted = list_ref[0, l]
        octant = jnp.where(entry == l, wanted % per_region, octant)
        region = jnp.where(entry == l, wanted // per_region, region)
    source = (cell * regions + region) * 4
    columns = iota((rows, devices * 4), 1)
    flat = packs_ref[...].reshape(devices * 4, packs_ref.shape[2])
    coarse = dot((columns == source + comp).astype(BF16), flat)
    marks = dot((columns == source + 3).astype(BF16), flat)
    inside = (marks[:, nb : 2 * nb] == octant.astype(F32)).astype(BF16)
    widen = (iota((nb, fine), 0) == iota((nb, fine), 1) // blk).astype(BF16)
    inside = dot(inside, widen)
    forces = dot(coarse.astype(BF16), bend_ref[...]).astype(BF16).astype(F32)
    arriving.wait(0)
    density = dot_lanes((forces * inside).astype(BF16), dens_ref[...])
    span = 3 * listed
    density = sum(density[c * span : (c + 1) * span] for c in range(cells)).astype(BF16)
    arriving.wait(1)
    expansion = sum(
        dot(density[k * listed : (k + 1) * listed], trans_ref[k * points : (k + 1) * points, :])
        for k in range(3)
    )
    far = jnp.sum(expansion.astype(BF16).astype(F32), axis=0, keepdims=True)
    far = jnp.concatenate(
        [far[:, k * points : (k + 1) * points] for k in range(3)] + [jnp.zeros((1, points), F32)],
        axis=0,
    )
    arriving.wait(2)
    total = near_ref[0:4, :] + dot(far.astype(BF16), eval_ref[...])
    arriving.wait(3)
    velocity = dot_lanes(total.astype(BF16), smooth_ref[...])
    for k in range(3):
        out_ref[k] = velocity[k : k + 1]


def in_place(x):
    return pltpu.with_memory_space_constraint(x, pltpu.HBM)


def vmem(megabytes):
    return pltpu.CompilerParams(vmem_limit_bytes=megabytes << 20)


def on_device(
    cell_shape,
    upsample,
    bending,
    to_density,
    translate,
    evaluate,
    smoothing,
    block_owner,
    block_octant,
    far_list,
):
    cells, regions = lax.axis_size("cells"), lax.axis_size("region")
    coarse, fine = upsample.shape
    nb = block_owner.shape[0]
    blk = fine // nb
    own_cell, own_blocks = cell_shape.reshape(3, coarse), block_owner.reshape(1, nb)
    pack, spread = pl.pallas_call(
        pack_kernel,
        out_shape=(
            jax.ShapeDtypeStruct((4, coarse), BF16),
            jax.ShapeDtypeStruct((cells * regions, 4, coarse), BF16),
        ),
        cost_estimate=pl.CostEstimate(flops=5 * 10**10, bytes_accessed=10**6, transcendentals=0),
        name="pack",
    )(own_cell, own_blocks, block_octant)
    others = [
        lax.ppermute(pack, "cells", [(i, i ^ k) for i in range(cells)])
        for k in sorted(range(1, cells), reverse=True)
    ]
    everyone = lax.all_to_all(spread, ("cells", "region"), split_axis=0, concat_axis=0, tiled=True)
    in_vmem = pl.BlockSpec(memory_space=pltpu.VMEM)
    in_hbm = pl.BlockSpec(memory_space=pltpu.HBM)
    points = cells * (nb // cells + 2) * blk
    near = pl.pallas_call(
        functools.partial(near_kernel, blk, len(others)),
        out_shape=jax.ShapeDtypeStruct((4, fine), F32),
        in_specs=[in_vmem] * (cells + 2) + [in_hbm],
        scratch_shapes=[
            pltpu.VMEM(upsample.shape, BF16),
            pltpu.VMEM((cells, 8, points), F32),
            pltpu.VMEM((cells, 4 * blk, points // (cells * blk)), F32),
            pltpu.SemaphoreType.DMA((1, len(row_chunks(coarse)))),
        ],
        compiler_params=vmem(40),
        cost_estimate=pl.CostEstimate(flops=5 * 10**10, bytes_accessed=10**6, transcendentals=0),
        name="near",
    )(own_cell, own_blocks, *others, bending, in_place(upsample))
    later = [in_place(x) for x in (to_density.T, translate, evaluate, smoothing.T)]
    velocity = pl.pallas_call(
        functools.partial(far_kernel, blk, cells, regions),
        out_shape=jax.ShapeDtypeStruct((3, 1, coarse), F32),
        in_specs=[pl.BlockSpec(memory_space=pltpu.SMEM)] + [in_vmem] * 3 + [in_hbm] * 4,
        scratch_shapes=[pltpu.VMEM(x.shape, BF16) for x in later]
        + [pltpu.SemaphoreType.DMA((4, len(row_chunks(coarse))))],
        compiler_params=vmem(32),
        name="far",
    )(far_list, everyone, near, bending, *later)
    return velocity.transpose(1, 0, 2)


def solution(mesh):
    own = P(("cells", "region"))
    return jax.shard_map(
        on_device,
        mesh=mesh,
        in_specs=(own, P(), P(), P(), P(), P(), P(), own, own, own),
        out_specs=own,
        check_vma=False,
    )
```

```python
import functools

import jax
import jax.numpy as jnp
from jax import lax
from jax.experimental import pallas as pl
from jax.experimental.pallas import tpu as pltpu
from jax.sharding import PartitionSpec as P

EPSILON_SQ = 0.0625
STOKES_SCALE = 1.0 / (8.0 * 3.141592653589793)
EXPAND_LIMIT = 128.0
TILE = 256
OCTANTS_PER_OWNER = 2
COPY_TILES = 3
F32 = jnp.float32
BF16 = jnp.bfloat16
LANES = (((1,), (1,)), ((), ()))


def iota(shape, dim):
    return lax.broadcasted_iota(jnp.int32, shape, dim)


def dot(a, b):
    return jnp.dot(a, b, preferred_element_type=F32)


def dot_lanes(a, b):
    return lax.dot_general(a, b, LANES, preferred_element_type=F32)


def split_bf16(x):
    high = x.astype(BF16)
    return high, (x - high.astype(F32)).astype(BF16)


def lane_chunks(lanes, tiles):
    return [(start, min(start + tiles * TILE, lanes)) for start in range(0, lanes, tiles * TILE)]


def in_stages(*stages):
    def step(at, _):
        for n, stage in enumerate(stages):
            pl.when(at == n)(stage)
        return 0

    lax.fori_loop(0, len(stages), step, 0)


def pack_kernel(cell_ref, owner_ref, octant_ref, pack_ref, spread_ref):
    nb = owner_ref.shape[1]
    width = cell_ref.shape[1]
    octant = octant_ref[...].reshape(1, nb)
    pack_ref[0:3, :] = cell_ref[...]
    row = jnp.concatenate(
        [
            owner_ref[...].astype(F32),
            octant.astype(F32),
            jnp.zeros((1, width - 2 * nb), F32),
        ],
        axis=1,
    )
    pack_ref[3:4, :] = row.astype(BF16)
    spread_ref[...] = jnp.broadcast_to(pack_ref[...][None], spread_ref.shape)


def interleave_matrix(blk):
    group = TILE // blk
    point, lane = iota((TILE, TILE), 0), iota((TILE, TILE), 1)
    return ((point % blk == lane // group) & (point // blk == lane % group)).astype(BF16)


def source_columns(rows):
    forces = jnp.concatenate([rows[4:8], rows[4:8]], axis=0)
    places = jnp.concatenate([rows[0:4], rows[0:4]], axis=0)
    upper = iota(rows.shape, 0) < 4
    groups = []
    square = jnp.zeros_like(rows)
    inner = jnp.zeros_like(rows)
    for k in range(3):
        x_k = jnp.broadcast_to(rows[k : k + 1], rows.shape)
        product = x_k * forces
        high = product.astype(BF16).astype(F32)
        groups.append(jnp.where(upper, high, product - high))
        square = square + x_k * x_k
        inner = inner + x_k * rows[4 + k : 5 + k]
    rest = square * forces + inner * places
    high = rest.astype(BF16).astype(F32)
    middle = (rest - high).astype(BF16).astype(F32)
    groups.append(jnp.where(upper, high, middle))
    groups.append(jnp.where(upper, rest - high - middle, forces))
    return jnp.concatenate(groups, axis=0).astype(BF16)


def three_parts(x):
    high = x.astype(BF16).astype(F32)
    middle = (x - high).astype(BF16).astype(F32)
    return high, middle, x - high - middle


def distance_factors(rows, targets):
    def side(points, scale, extra, squares_first):
        square = jnp.sum(jnp.square(points[0:4]), axis=0, keepdims=True) + extra
        ones = [jnp.ones_like(square)] * 3
        squares = list(three_parts(square))
        parts = squares + ones if squares_first else ones + squares
        unused = jnp.zeros((7, points.shape[1]), F32)
        return jnp.concatenate([points[0:3] * scale] + parts + [unused], axis=0)

    source = side(rows, -2.0, 0.0, False).astype(BF16)
    target = side(targets, 1.0, EPSILON_SQ, True).T.astype(BF16)
    return source, target


def expanded_sums(rows, targets):
    columns = source_columns(rows)
    source, target = distance_factors(rows, targets)
    inverse = lax.rsqrt(dot(target, source))
    cubed = (inverse * inverse * inverse).astype(BF16)
    sums = dot_lanes(columns, cubed)
    place = targets[0:4]
    moment = [sums[8 * k : 8 * k + 4] + sums[8 * k + 4 : 8 * k + 8] for k in range(3)]
    rest = sums[24:28] + sums[28:32] + sums[32:36]
    force = sums[36:40]
    square = jnp.sum(place * place, axis=0, keepdims=True)
    along = jnp.sum(place * force, axis=0, keepdims=True)
    trace = moment[0][0:1] + moment[1][1:2] + moment[2][2:3]
    cross = [jnp.sum(place * moment[k], axis=0, keepdims=True) for k in range(3)]
    cross = jnp.concatenate(cross + [jnp.zeros_like(trace)], axis=0)
    weighted = place[0:1] * moment[0] + place[1:2] * moment[1] + place[2:3] * moment[2]
    return (
        (square + 2.0 * EPSILON_SQ) * force + rest - 2.0 * weighted + place * (along - trace) - cross
    )


def direct_sums(rows, targets):
    strength = rows[4:8].astype(BF16)
    ones = jnp.ones((1, rows.shape[1]), F32)
    places = jnp.concatenate([rows[0:3], ones], axis=0).astype(BF16)
    upright = targets.T
    sums = None
    for start in range(0, rows.shape[1], TILE):
        stop = min(start + TILE, rows.shape[1])
        diffs = [upright[:, k : k + 1] - rows[k : k + 1, start:stop] for k in range(3)]
        dist = diffs[0] * diffs[0] + diffs[1] * diffs[1] + diffs[2] * diffs[2] + EPSILON_SQ
        inverse = lax.rsqrt(dist)
        cubed = inverse * inverse * inverse
        direct = ((dist + EPSILON_SQ) * cubed).astype(BF16)
        along = sum(diffs[k] * rows[4 + k : 5 + k, start:stop] for k in range(3))
        radial = (along * cubed).astype(BF16)
        near = dot_lanes(strength[:, start:stop], direct)
        away = dot_lanes(places[:, start:stop], radial)
        part = jnp.concatenate([near, away], axis=0)
        sums = part if sums is None else sums + part
    return sums[0:4] + targets[0:4] * sums[7:8] - sums[4:8]


def near_kernel(blk, packs_given, *refs):
    cell_ref, owner_ref, *pack_refs = refs[: packs_given + 2]
    bend_ref, up_hbm, out_ref, up_ref, *refs = refs[packs_given + 2 :]
    places_ref, bent_ref, sort_ref, part_ref, rows_ref, found_ref, sems = refs
    chunks = lane_chunks(up_ref.shape[1], COPY_TILES)
    copies = [
        pltpu.make_async_copy(up_hbm.at[:, a:b], up_ref.at[:, a:b], sems.at[n])
        for n, (a, b) in enumerate(chunks)
    ]
    for copy in copies:
        copy.start()
    cells = packs_given + 1
    fine = up_ref.shape[1]
    nb = fine // blk
    capacity = nb // cells + 2
    spots = cells * capacity
    group = TILE // blk
    tiles = -(-fine // TILE)

    def prepare():
        packs = [ref[...].astype(F32) for ref in pack_refs]
        none = jnp.zeros((1, cell_ref.shape[1]), F32)
        coarse = [jnp.concatenate([cell_ref[...].astype(F32), none], axis=0)]
        coarse += [jnp.where(iota(pack.shape, 0) < 3, pack, 0.0) for pack in packs]
        owners = [owner_ref[...].astype(F32)] + [pack[3:4, 0:nb] for pack in packs]
        point_rows, force_rows = [], []
        for three in coarse:
            point_rows += [three, jnp.zeros_like(three)]
            force_rows += [jnp.zeros_like(three), three]
        places_ref[...] = jnp.concatenate(point_rows, axis=0).astype(BF16)
        force_rows = jnp.concatenate(force_rows, axis=0).astype(BF16)
        bent_ref[...] = dot(force_rows, bend_ref[...])
        leaf_ids = iota((cells, nb), 0).astype(F32)
        chosen = jnp.concatenate([(leaf_ids == own).astype(F32) for own in owners], axis=0)
        earlier = (iota((nb, nb), 0) < iota((nb, nb), 1)).astype(BF16)
        before = dot(chosen.astype(BF16), earlier) * chosen
        spot_ids = iota((spots, nb), 0).astype(F32)
        for c in range(cells):
            rank = jnp.sum(before[c * cells : (c + 1) * cells], axis=0, keepdims=True)
            sort_ref[c] = (spot_ids == owners[c] * capacity + rank).astype(BF16)

    def part_points(n):
        a, b = chunks[n]
        copies[n].wait()
        fields = (bent_ref[:, a:b] + dot(places_ref[...], up_ref[:, a:b])).astype(BF16)
        if (b - a) % TILE:
            rest = jnp.zeros((8 * cells, -(b - a) % TILE), BF16)
            fields = jnp.concatenate([fields, rest], axis=1)
        stacked = [fields[:, t : t + TILE] for t in range(0, fields.shape[1], TILE)]
        parted = dot(jnp.concatenate(stacked, axis=0), interleave_matrix(blk))
        first = a // TILE * 8 * cells
        part_ref[first : first + parted.shape[0]] = parted

    def finish():
        near_sums(blk, cells, fine, out_ref, sort_ref, part_ref, rows_ref, found_ref)

    in_stages(
        prepare, *[functools.partial(part_points, n) for n in range(len(chunks))], finish
    )


def near_sums(blk, cells, fine, out_ref, sort_ref, part_ref, rows_ref, found_ref):
    nb = fine // blk
    capacity = nb // cells + 2
    group = TILE // blk
    tiles = -(-fine // TILE)
    mix = interleave_matrix(blk)
    parted = part_ref[...]
    sorts = [sort_ref[c] for c in range(cells)]
    by_point = [
        jnp.concatenate(
            [
                parted[t * 8 * cells : (t + 1) * 8 * cells, k * group : (k + 1) * group]
                for t in range(tiles)
            ],
            axis=1,
        )[:, 0:nb]
        for k in range(blk)
    ]
    by_leaf = []
    for c in range(cells):
        rows = jnp.concatenate([by_point[k][8 * c : 8 * c + 8] for k in range(blk)], axis=0)
        by_leaf.append(dot_lanes(rows.astype(BF16), sorts[c]))
    for leaf in range(cells):
        rows_ref[leaf] = jnp.concatenate(
            [
                by_leaf[c][8 * k : 8 * k + 8, leaf * capacity : (leaf + 1) * capacity]
                for c in range(cells)
                for k in range(blk)
            ],
            axis=1,
        )
    farthest = jnp.max(
        sum(jnp.square(by_leaf[c][8 * k : 8 * k + 4]) for c in range(cells) for k in range(blk))
    )

    def each_leaf(sums, leaf, _):
        rows = rows_ref[leaf]
        velocity = sums(rows, rows[:, 0 : capacity * blk]) * STOKES_SCALE
        found_ref[leaf] = jnp.concatenate(
            [velocity[:, k * capacity : (k + 1) * capacity] for k in range(blk)], axis=0
        )
        return 0

    lax.fori_loop(0, cells, functools.partial(each_leaf, expanded_sums), 0, unroll=cells <= 4)

    @pl.when(farthest > EXPAND_LIMIT)
    def _():
        lax.fori_loop(0, cells, functools.partial(each_leaf, direct_sums), 0)

    found = jnp.concatenate([found_ref[leaf] for leaf in range(cells)], axis=1)
    high, low = split_bf16(found)
    back = dot(jnp.concatenate([high, low], axis=0), sorts[0])
    back = back[: 4 * blk] + back[4 * blk :]
    back = jnp.concatenate([back, jnp.zeros((4 * blk, tiles * group - nb), F32)], axis=1)
    pieces = [
        jnp.concatenate(
            [back[4 * k : 4 * k + 4, t * group : (t + 1) * group] for k in range(blk)], axis=1
        )
        for t in range(tiles)
    ]
    high, low = split_bf16(jnp.concatenate(pieces, axis=0))
    natural = dot_lanes(high, mix) + dot_lanes(low, mix)
    for t in range(tiles):
        stop = min((t + 1) * TILE, fine)
        out_ref[0:4, t * TILE : stop] = natural[4 * t : 4 * t + 4, 0 : stop - t * TILE]

def far_kernel(blk, cells, regions, *refs):
    list_ref, packs_ref, near_ref, bend_ref, dens_ref, *in_hbm = refs[:8]
    out_ref, trans_ref, eval_ref, smooth_ref, density_ref, total_ref, sems = refs[8:]
    trans_copy, eval_copy, smooth_copy = [
        pltpu.make_async_copy(src, dst, sems.at[n])
        for n, (src, dst) in enumerate(zip(in_hbm, (trans_ref, eval_ref, smooth_ref)))
    ]
    for copy in (trans_copy, eval_copy, smooth_copy):
        copy.start()
    listed = list_ref.shape[1]
    fine = bend_ref.shape[1]
    nb = fine // blk
    points = eval_ref.shape[0]
    per_region = OCTANTS_PER_OWNER * cells
    rows = cells * 3 * listed
    devices = cells * regions
    span = 3 * listed

    def densities():
        row = iota((rows, 1), 0)
        entry, comp, cell = row % listed, row // listed % 3, row // span
        octant = jnp.zeros((rows, 1), jnp.int32)
        region = jnp.zeros((rows, 1), jnp.int32)
        for l in range(listed):
            wanted = list_ref[0, l]
            octant = jnp.where(entry == l, wanted % per_region, octant)
            region = jnp.where(entry == l, wanted // per_region, region)
        source = (cell * regions + region) * 4
        columns = iota((rows, devices * 4), 1)
        flat = packs_ref[...].reshape(devices * 4, packs_ref.shape[2])
        coarse = dot((columns == source + comp).astype(BF16), flat)
        marks = dot((columns == source + 3).astype(BF16), flat)
        inside = (marks[:, nb : 2 * nb] == octant.astype(F32)).astype(BF16)
        widen = (iota((nb, fine), 0) == iota((nb, fine), 1) // blk).astype(BF16)
        inside = dot(inside, widen)
        forces = dot(coarse.astype(BF16), bend_ref[...]).astype(BF16).astype(F32)
        density = dot_lanes((forces * inside).astype(BF16), dens_ref[...])
        density_ref[...] = sum(density[c * span : (c + 1) * span] for c in range(cells))

    def totals():
        trans_copy.wait()
        eval_copy.wait()
        density = density_ref[...].astype(BF16)
        expansion = sum(
            dot(density[k * listed : (k + 1) * listed], trans_ref[k * points : (k + 1) * points, :])
            for k in range(3)
        )
        far = jnp.sum(expansion.astype(BF16).astype(F32), axis=0, keepdims=True)
        far = jnp.concatenate(
            [far[:, k * points : (k + 1) * points] for k in range(3)]
            + [jnp.zeros((1, points), F32)],
            axis=0,
        )
        total_ref[...] = near_ref[0:4, :] + dot(far.astype(BF16), eval_ref[...])

    def velocities():
        smooth_copy.wait()
        velocity = dot_lanes(total_ref[...].astype(BF16), smooth_ref[...])
        for k in range(3):
            out_ref[k] = velocity[k : k + 1]

    in_stages(densities, totals, velocities)


def in_place(x):
    return pltpu.with_memory_space_constraint(x, pltpu.HBM)


def vmem(megabytes):
    return pltpu.CompilerParams(vmem_limit_bytes=megabytes << 20)


def on_device(
    cell_shape,
    upsample,
    bending,
    to_density,
    translate,
    evaluate,
    smoothing,
    block_owner,
    block_octant,
    far_list,
):
    cells, regions = lax.axis_size("cells"), lax.axis_size("region")
    coarse, fine = upsample.shape
    nb = block_owner.shape[0]
    blk = fine // nb
    own_cell, own_blocks = cell_shape.reshape(3, coarse), block_owner.reshape(1, nb)
    pack, spread = pl.pallas_call(
        pack_kernel,
        out_shape=(
            jax.ShapeDtypeStruct((4, coarse), BF16),
            jax.ShapeDtypeStruct((cells * regions, 4, coarse), BF16),
        ),
        cost_estimate=pl.CostEstimate(flops=5 * 10**10, bytes_accessed=10**6, transcendentals=0),
        name="pack",
    )(own_cell, own_blocks, block_octant)
    others = [
        lax.ppermute(pack, "cells", [(i, i ^ k) for i in range(cells)])
        for k in sorted(range(1, cells), reverse=True)
    ]
    everyone = lax.all_to_all(spread, ("cells", "region"), split_axis=0, concat_axis=0, tiled=True)
    in_vmem = pl.BlockSpec(memory_space=pltpu.VMEM)
    in_hbm = pl.BlockSpec(memory_space=pltpu.HBM)
    points = cells * (nb // cells + 2) * blk
    near = pl.pallas_call(
        functools.partial(near_kernel, blk, len(others)),
        out_shape=jax.ShapeDtypeStruct((4, fine), F32),
        in_specs=[in_vmem] * (cells + 2) + [in_hbm],
        scratch_shapes=[
            pltpu.VMEM(upsample.shape, BF16),
            pltpu.VMEM((8 * cells, coarse), BF16),
            pltpu.VMEM((8 * cells, fine), F32),
            pltpu.VMEM((cells, points // blk, nb), BF16),
            pltpu.VMEM((-(-fine // TILE) * 8 * cells, TILE), F32),
            pltpu.VMEM((cells, 8, points), F32),
            pltpu.VMEM((cells, 4 * blk, points // (cells * blk)), F32),
            pltpu.SemaphoreType.DMA((len(lane_chunks(fine, COPY_TILES)),)),
        ],
        compiler_params=vmem(40),
        cost_estimate=pl.CostEstimate(flops=5 * 10**10, bytes_accessed=10**6, transcendentals=0),
        name="near",
    )(own_cell, own_blocks, *others, bending, in_place(upsample))
    later = [in_place(x) for x in (translate, evaluate, smoothing.T)]
    velocity = pl.pallas_call(
        functools.partial(far_kernel, blk, cells, regions),
        out_shape=jax.ShapeDtypeStruct((3, 1, coarse), F32),
        in_specs=[pl.BlockSpec(memory_space=pltpu.SMEM)] + [in_vmem] * 4 + [in_hbm] * 3,
        scratch_shapes=[pltpu.VMEM(x.shape, BF16) for x in later]
        + [
            pltpu.VMEM((3 * far_list.shape[1], evaluate.shape[0]), F32),
            pltpu.VMEM((4, fine), F32),
            pltpu.SemaphoreType.DMA((3,)),
        ],
        compiler_params=vmem(32),
        name="far",
    )(far_list, everyone, near, bending, to_density.T, *later)
    return velocity.transpose(1, 0, 2)


def solution(mesh):
    own = P(("cells", "region"))
    return jax.shard_map(
        on_device,
        mesh=mesh,
        in_specs=(own, P(), P(), P(), P(), P(), P(), own, own, own),
        out_specs=own,
        check_vma=False,
    )
```

```python
import functools

import jax
import jax.numpy as jnp
from jax import lax
from jax.experimental import pallas as pl
from jax.experimental.pallas import tpu as pltpu
from jax.sharding import PartitionSpec as P

EPSILON_SQ = 0.0625
STOKES_SCALE = 1.0 / (8.0 * 3.141592653589793)
EXPAND_LIMIT = 128.0
TILE = 256
OCTANTS_PER_OWNER = 2
COPY_TILES = 3
SOURCE_TILES = 5
F32 = jnp.float32
BF16 = jnp.bfloat16
LANES = (((1,), (1,)), ((), ()))


def iota(shape, dim):
    return lax.broadcasted_iota(jnp.int32, shape, dim)


def dot(a, b):
    return jnp.dot(a, b, preferred_element_type=F32)


def dot_lanes(a, b):
    return lax.dot_general(a, b, LANES, preferred_element_type=F32)


def split_bf16(x):
    high = x.astype(BF16)
    return high, (x - high.astype(F32)).astype(BF16)


def lane_chunks(lanes, tiles):
    return [(start, min(start + tiles * TILE, lanes)) for start in range(0, lanes, tiles * TILE)]


def in_stages(*stages):
    def step(at, _):
        for n, stage in enumerate(stages):
            pl.when(at == n)(stage)
        return 0

    lax.fori_loop(0, len(stages), step, 0)


def spread_rows(coarse, nb):
    whole, rest = coarse // TILE, coarse % TILE
    return whole, rest, 3 * whole + -(-(3 * rest + nb) // TILE)


def pack_kernel(cell_ref, owner_ref, octant_ref, pack_ref, spread_ref):
    nb = owner_ref.shape[1]
    coarse = cell_ref.shape[1]
    whole, rest, height = spread_rows(coarse, nb)
    cell = cell_ref[...].astype(F32)
    owner = jnp.concatenate(
        [owner_ref[...].astype(F32), jnp.zeros((1, coarse - nb), F32)], axis=1
    )
    pack_ref[...] = jnp.concatenate([cell, owner], axis=0).astype(BF16)
    rows = [cell[k : k + 1, t * TILE : (t + 1) * TILE] for k in range(3) for t in range(whole)]
    tail = [cell[k : k + 1, whole * TILE :] for k in range(3)]
    tail.append(octant_ref[...].reshape(1, nb).astype(F32))
    tail.append(jnp.zeros((1, (height - 3 * whole) * TILE - 3 * rest - nb), F32))
    tail = jnp.concatenate(tail, axis=1)
    rows += [tail[:, t : t + TILE] for t in range(0, tail.shape[1], TILE)]
    rows = jnp.concatenate(rows, axis=0).astype(BF16)
    spread_ref[...] = jnp.broadcast_to(rows[None], spread_ref.shape)


def interleave_matrix(blk):
    group = TILE // blk
    point, lane = iota((TILE, TILE), 0), iota((TILE, TILE), 1)
    return ((point % blk == lane // group) & (point // blk == lane % group)).astype(BF16)


def source_columns(rows):
    forces = jnp.concatenate([rows[4:8], rows[4:8]], axis=0)
    places = jnp.concatenate([rows[0:4], rows[0:4]], axis=0)
    upper = iota(rows.shape, 0) < 4
    groups = []
    square = jnp.zeros_like(rows)
    inner = jnp.zeros_like(rows)
    for k in range(3):
        x_k = jnp.broadcast_to(rows[k : k + 1], rows.shape)
        product = x_k * forces
        high = product.astype(BF16).astype(F32)
        groups.append(jnp.where(upper, high, product - high))
        square = square + x_k * x_k
        inner = inner + x_k * rows[4 + k : 5 + k]
    rest = square * forces + inner * places
    high = rest.astype(BF16).astype(F32)
    middle = (rest - high).astype(BF16).astype(F32)
    groups.append(jnp.where(upper, high, middle))
    groups.append(jnp.where(upper, rest - high - middle, forces))
    return jnp.concatenate(groups, axis=0).astype(BF16)


def three_parts(x):
    high = x.astype(BF16).astype(F32)
    middle = (x - high).astype(BF16).astype(F32)
    return high, middle, x - high - middle


def distance_factors(rows, targets):
    def side(points, scale, extra, squares_first):
        square = jnp.sum(jnp.square(points[0:4]), axis=0, keepdims=True) + extra
        ones = [jnp.ones_like(square)] * 3
        squares = list(three_parts(square))
        parts = squares + ones if squares_first else ones + squares
        unused = jnp.zeros((7, points.shape[1]), F32)
        return jnp.concatenate([points[0:3] * scale] + parts + [unused], axis=0)

    source = side(rows, -2.0, 0.0, False).astype(BF16)
    target = side(targets, 1.0, EPSILON_SQ, True).T.astype(BF16)
    return source, target


def expanded_sums(rows, targets):
    columns = source_columns(rows)
    source, target = distance_factors(rows, targets)
    sums = None
    for start in range(0, rows.shape[1], SOURCE_TILES * TILE):
        part = slice(start, min(start + SOURCE_TILES * TILE, rows.shape[1]))
        inverse = lax.rsqrt(dot(target, source[:, part]))
        cubed = (inverse * inverse * inverse).astype(BF16)
        some = dot_lanes(columns[:, part], cubed)
        sums = some if sums is None else sums + some
    place = targets[0:4]
    moment = [sums[8 * k : 8 * k + 4] + sums[8 * k + 4 : 8 * k + 8] for k in range(3)]
    rest = sums[24:28] + sums[28:32] + sums[32:36]
    force = sums[36:40]
    square = jnp.sum(place * place, axis=0, keepdims=True)
    along = jnp.sum(place * force, axis=0, keepdims=True)
    trace = moment[0][0:1] + moment[1][1:2] + moment[2][2:3]
    cross = [jnp.sum(place * moment[k], axis=0, keepdims=True) for k in range(3)]
    cross = jnp.concatenate(cross + [jnp.zeros_like(trace)], axis=0)
    weighted = place[0:1] * moment[0] + place[1:2] * moment[1] + place[2:3] * moment[2]
    return (
        (square + 2.0 * EPSILON_SQ) * force + rest - 2.0 * weighted + place * (along - trace) - cross
    )


def direct_sums(rows, targets):
    strength = rows[4:8].astype(BF16)
    ones = jnp.ones((1, rows.shape[1]), F32)
    places = jnp.concatenate([rows[0:3], ones], axis=0).astype(BF16)
    upright = targets.T
    sums = None
    for start in range(0, rows.shape[1], TILE):
        stop = min(start + TILE, rows.shape[1])
        diffs = [upright[:, k : k + 1] - rows[k : k + 1, start:stop] for k in range(3)]
        dist = diffs[0] * diffs[0] + diffs[1] * diffs[1] + diffs[2] * diffs[2] + EPSILON_SQ
        inverse = lax.rsqrt(dist)
        cubed = inverse * inverse * inverse
        direct = ((dist + EPSILON_SQ) * cubed).astype(BF16)
        along = sum(diffs[k] * rows[4 + k : 5 + k, start:stop] for k in range(3))
        radial = (along * cubed).astype(BF16)
        near = dot_lanes(strength[:, start:stop], direct)
        away = dot_lanes(places[:, start:stop], radial)
        part = jnp.concatenate([near, away], axis=0)
        sums = part if sums is None else sums + part
    return sums[0:4] + targets[0:4] * sums[7:8] - sums[4:8]


def near_kernel(blk, packs_given, *refs):
    cell_ref, owner_ref, *pack_refs = refs[: packs_given + 2]
    bend_ref, up_hbm, out_ref, up_ref, *refs = refs[packs_given + 2 :]
    places_ref, bent_ref, sort_ref, part_ref, rows_ref, found_ref, sems = refs
    chunks = lane_chunks(up_ref.shape[1], COPY_TILES)
    copies = [
        pltpu.make_async_copy(up_hbm.at[:, a:b], up_ref.at[:, a:b], sems.at[n])
        for n, (a, b) in enumerate(chunks)
    ]
    for copy in copies:
        copy.start()
    cells = packs_given + 1
    fine = up_ref.shape[1]
    nb = fine // blk
    capacity = nb // cells + 2
    spots = cells * capacity
    group = TILE // blk
    tiles = -(-fine // TILE)

    def prepare():
        packs = [ref[...].astype(F32) for ref in pack_refs]
        none = jnp.zeros((1, cell_ref.shape[1]), F32)
        coarse = [jnp.concatenate([cell_ref[...].astype(F32), none], axis=0)]
        coarse += [jnp.where(iota(pack.shape, 0) < 3, pack, 0.0) for pack in packs]
        owners = [owner_ref[...].astype(F32)] + [pack[3:4, 0:nb] for pack in packs]
        point_rows, force_rows = [], []
        for three in coarse:
            point_rows += [three, jnp.zeros_like(three)]
            force_rows += [jnp.zeros_like(three), three]
        places_ref[...] = jnp.concatenate(point_rows, axis=0).astype(BF16)
        force_rows = jnp.concatenate(force_rows, axis=0).astype(BF16)
        bent_ref[...] = dot(force_rows, bend_ref[...])
        leaf_ids = iota((cells, nb), 0).astype(F32)
        chosen = jnp.concatenate([(leaf_ids == own).astype(F32) for own in owners], axis=0)
        earlier = (iota((nb, nb), 0) < iota((nb, nb), 1)).astype(BF16)
        before = dot(chosen.astype(BF16), earlier) * chosen
        spot_ids = iota((spots, nb), 0).astype(F32)
        for c in range(cells):
            rank = jnp.sum(before[c * cells : (c + 1) * cells], axis=0, keepdims=True)
            sort_ref[c] = (spot_ids == owners[c] * capacity + rank).astype(BF16)

    def part_points(n):
        a, b = chunks[n]
        copies[n].wait()
        fields = (bent_ref[:, a:b] + dot(places_ref[...], up_ref[:, a:b])).astype(BF16)
        if (b - a) % TILE:
            rest = jnp.zeros((8 * cells, -(b - a) % TILE), BF16)
            fields = jnp.concatenate([fields, rest], axis=1)
        stacked = [fields[:, t : t + TILE] for t in range(0, fields.shape[1], TILE)]
        parted = dot(jnp.concatenate(stacked, axis=0), interleave_matrix(blk))
        first = a // TILE * 8 * cells
        part_ref[first : first + parted.shape[0]] = parted

    def finish():
        near_sums(blk, cells, fine, out_ref, sort_ref, part_ref, rows_ref, found_ref)

    in_stages(
        prepare, *[functools.partial(part_points, n) for n in range(len(chunks))], finish
    )


def near_sums(blk, cells, fine, out_ref, sort_ref, part_ref, rows_ref, found_ref):
    nb = fine // blk
    capacity = nb // cells + 2
    group = TILE // blk
    tiles = -(-fine // TILE)
    mix = interleave_matrix(blk)
    parted = part_ref[...]
    sorts = [sort_ref[c] for c in range(cells)]
    by_point = [
        jnp.concatenate(
            [
                parted[t * 8 * cells : (t + 1) * 8 * cells, k * group : (k + 1) * group]
                for t in range(tiles)
            ],
            axis=1,
        )[:, 0:nb]
        for k in range(blk)
    ]
    by_leaf = []
    for c in range(cells):
        rows = jnp.concatenate([by_point[k][8 * c : 8 * c + 8] for k in range(blk)], axis=0)
        by_leaf.append(dot_lanes(rows.astype(BF16), sorts[c]))
    for leaf in range(cells):
        rows_ref[leaf] = jnp.concatenate(
            [
                by_leaf[c][8 * k : 8 * k + 8, leaf * capacity : (leaf + 1) * capacity]
                for c in range(cells)
                for k in range(blk)
            ],
            axis=1,
        )
    farthest = jnp.max(
        sum(jnp.square(by_leaf[c][8 * k : 8 * k + 4]) for c in range(cells) for k in range(blk))
    )

    def each_leaf(sums, leaf, _):
        rows = rows_ref[leaf]
        velocity = sums(rows, rows[:, 0 : capacity * blk]) * STOKES_SCALE
        found_ref[leaf] = jnp.concatenate(
            [velocity[:, k * capacity : (k + 1) * capacity] for k in range(blk)], axis=0
        )
        return 0

    lax.fori_loop(0, cells, functools.partial(each_leaf, expanded_sums), 0, unroll=cells <= 4)

    @pl.when(farthest > EXPAND_LIMIT)
    def _():
        lax.fori_loop(0, cells, functools.partial(each_leaf, direct_sums), 0)

    found = jnp.concatenate([found_ref[leaf] for leaf in range(cells)], axis=1)
    high, low = split_bf16(found)
    back = dot(jnp.concatenate([high, low], axis=0), sorts[0])
    back = back[: 4 * blk] + back[4 * blk :]
    back = jnp.concatenate([back, jnp.zeros((4 * blk, tiles * group - nb), F32)], axis=1)
    pieces = [
        jnp.concatenate(
            [back[4 * k : 4 * k + 4, t * group : (t + 1) * group] for k in range(blk)], axis=1
        )
        for t in range(tiles)
    ]
    high, low = split_bf16(jnp.concatenate(pieces, axis=0))
    natural = dot_lanes(high, mix) + dot_lanes(low, mix)
    for t in range(tiles):
        stop = min((t + 1) * TILE, fine)
        out_ref[0:4, t * TILE : stop] = natural[4 * t : 4 * t + 4, 0 : stop - t * TILE]

def far_kernel(blk, cells, regions, *refs):
    list_ref, packs_ref, near_ref, bend_ref, dens_ref, *in_hbm = refs[:8]
    out_ref, trans_ref, eval_ref, smooth_ref, density_ref, total_ref, sems = refs[8:]
    trans_copy, eval_copy, smooth_copy = [
        pltpu.make_async_copy(src, dst, sems.at[n])
        for n, (src, dst) in enumerate(zip(in_hbm, (trans_ref, eval_ref, smooth_ref)))
    ]
    for copy in (trans_copy, eval_copy, smooth_copy):
        copy.start()
    listed = list_ref.shape[1]
    fine = bend_ref.shape[1]
    nb = fine // blk
    points = eval_ref.shape[0]
    per_region = OCTANTS_PER_OWNER * cells
    rows = cells * 3 * listed
    devices = cells * regions
    span = 3 * listed
    whole, rest, height = spread_rows(bend_ref.shape[0], nb)

    def densities():
        row = iota((rows, 1), 0)
        entry, comp, cell = row % listed, row // listed % 3, row // span
        octant = jnp.zeros((rows, 1), jnp.int32)
        region = jnp.zeros((rows, 1), jnp.int32)
        for l in range(listed):
            wanted = list_ref[0:1, l : l + 1]
            octant = jnp.where(entry == l, wanted % per_region, octant)
            region = jnp.where(entry == l, wanted // per_region, region)
        source = (cell * regions + region) * height
        columns = iota((rows, devices * height), 1)
        flat = packs_ref[...].reshape(devices * height, TILE)

        def take(n):
            return dot((columns == source + n).astype(BF16), flat)

        coarse = [take(comp * whole + t) for t in range(whole)]
        tail = jnp.concatenate([take(n) for n in range(3 * whole, height)], axis=1)
        left = [tail[:, k * rest : (k + 1) * rest] for k in range(3)]
        coarse.append(jnp.where(comp == 0, left[0], jnp.where(comp == 1, left[1], left[2])))
        coarse = jnp.concatenate(coarse, axis=1)
        marks = tail[:, 3 * rest : 3 * rest + nb]
        inside = (marks == octant.astype(F32)).astype(BF16)
        widen = (iota((nb, fine), 0) == iota((nb, fine), 1) // blk).astype(BF16)
        inside = dot(inside, widen)
        forces = dot(coarse.astype(BF16), bend_ref[...]).astype(BF16).astype(F32)
        density = dot_lanes((forces * inside).astype(BF16), dens_ref[...])
        density_ref[...] = sum(density[c * span : (c + 1) * span] for c in range(cells))

    def totals():
        trans_copy.wait()
        eval_copy.wait()
        density = density_ref[...].astype(BF16)
        expansion = sum(
            dot(density[k * listed : (k + 1) * listed], trans_ref[k * points : (k + 1) * points, :])
            for k in range(3)
        )
        far = jnp.sum(expansion.astype(BF16).astype(F32), axis=0, keepdims=True)
        far = jnp.concatenate(
            [far[:, k * points : (k + 1) * points] for k in range(3)]
            + [jnp.zeros((1, points), F32)],
            axis=0,
        )
        total_ref[...] = near_ref[0:4, :] + dot(far.astype(BF16), eval_ref[...])

    def velocities():
        smooth_copy.wait()
        velocity = dot_lanes(total_ref[...].astype(BF16), smooth_ref[...])
        for k in range(3):
            out_ref[k] = velocity[k : k + 1]

    in_stages(densities, totals, velocities)


def in_place(x):
    return pltpu.with_memory_space_constraint(x, pltpu.HBM)


def vmem(megabytes):
    return pltpu.CompilerParams(vmem_limit_bytes=megabytes << 20)


def on_device(
    cell_shape,
    upsample,
    bending,
    to_density,
    translate,
    evaluate,
    smoothing,
    block_owner,
    block_octant,
    far_list,
):
    cells, regions = lax.axis_size("cells"), lax.axis_size("region")
    coarse, fine = upsample.shape
    nb = block_owner.shape[0]
    blk = fine // nb
    own_cell, own_blocks = cell_shape.reshape(3, coarse), block_owner.reshape(1, nb)
    pack, spread = pl.pallas_call(
        pack_kernel,
        out_shape=(
            jax.ShapeDtypeStruct((4, coarse), BF16),
            jax.ShapeDtypeStruct((cells * regions, spread_rows(coarse, nb)[2], TILE), BF16),
        ),
        cost_estimate=pl.CostEstimate(flops=5 * 10**10, bytes_accessed=10**6, transcendentals=0),
        name="pack",
    )(own_cell, own_blocks, block_octant)
    others = [
        lax.ppermute(pack, "cells", [(i, i ^ k) for i in range(cells)])
        for k in sorted(range(1, cells), reverse=True)
    ]
    everyone = lax.all_to_all(spread, ("cells", "region"), split_axis=0, concat_axis=0, tiled=True)
    in_vmem = pl.BlockSpec(memory_space=pltpu.VMEM)
    in_hbm = pl.BlockSpec(memory_space=pltpu.HBM)
    points = cells * (nb // cells + 2) * blk
    near = pl.pallas_call(
        functools.partial(near_kernel, blk, len(others)),
        out_shape=jax.ShapeDtypeStruct((4, fine), F32),
        in_specs=[in_vmem] * (cells + 2) + [in_hbm],
        scratch_shapes=[
            pltpu.VMEM(upsample.shape, BF16),
            pltpu.VMEM((8 * cells, coarse), BF16),
            pltpu.VMEM((8 * cells, fine), F32),
            pltpu.VMEM((cells, points // blk, nb), BF16),
            pltpu.VMEM((-(-fine // TILE) * 8 * cells, TILE), F32),
            pltpu.VMEM((cells, 8, points), F32),
            pltpu.VMEM((cells, 4 * blk, points // (cells * blk)), F32),
            pltpu.SemaphoreType.DMA((len(lane_chunks(fine, COPY_TILES)),)),
        ],
        compiler_params=vmem(40),
        cost_estimate=pl.CostEstimate(flops=5 * 10**10, bytes_accessed=10**6, transcendentals=0),
        name="near",
    )(own_cell, own_blocks, *others, bending, in_place(upsample))
    later = [in_place(x) for x in (translate, evaluate, smoothing.T)]
    velocity = pl.pallas_call(
        functools.partial(far_kernel, blk, cells, regions),
        out_shape=jax.ShapeDtypeStruct((3, 1, coarse), F32),
        in_specs=[in_vmem] * 5 + [in_hbm] * 3,
        scratch_shapes=[pltpu.VMEM(x.shape, BF16) for x in later]
        + [
            pltpu.VMEM((3 * far_list.shape[1], evaluate.shape[0]), F32),
            pltpu.VMEM((4, fine), F32),
            pltpu.SemaphoreType.DMA((3,)),
        ],
        compiler_params=vmem(32),
        name="far",
    )(far_list, everyone, near, bending, to_density.T, *later)
    return velocity.transpose(1, 0, 2)


def solution(mesh):
    own = P(("cells", "region"))
    return jax.shard_map(
        on_device,
        mesh=mesh,
        in_specs=(own, P(), P(), P(), P(), P(), P(), own, own, own),
        out_specs=own,
        check_vma=False,
    )
```

```python
import functools

import jax
import jax.numpy as jnp
from jax import lax
from jax.experimental import pallas as pl
from jax.experimental.pallas import tpu as pltpu
from jax.sharding import PartitionSpec as P

EPSILON_SQ = 0.0625
STOKES_SCALE = 1.0 / (8.0 * 3.141592653589793)
EXPAND_LIMIT = 128.0
TILE = 256
OCTANTS_PER_OWNER = 2
COPY_TILES = 3
SOURCE_TILES = 5
F32 = jnp.float32
BF16 = jnp.bfloat16
LANES = (((1,), (1,)), ((), ()))


def iota(shape, dim):
    return lax.broadcasted_iota(jnp.int32, shape, dim)


def dot(a, b):
    return jnp.dot(a, b, preferred_element_type=F32)


def dot_lanes(a, b):
    return lax.dot_general(a, b, LANES, preferred_element_type=F32)


def split_bf16(x):
    high = x.astype(BF16)
    return high, (x - high.astype(F32)).astype(BF16)


def lane_chunks(lanes, tiles):
    return [(start, min(start + tiles * TILE, lanes)) for start in range(0, lanes, tiles * TILE)]


def in_stages(*stages):
    def step(at, _):
        for n, stage in enumerate(stages):
            pl.when(at == n)(stage)
        return 0

    lax.fori_loop(0, len(stages), step, 0)


def spread_rows(coarse, nb):
    whole, rest = coarse // TILE, coarse % TILE
    return whole, rest, 3 * whole + -(-(3 * rest + nb) // TILE)


def pack_kernel(cell_ref, owner_ref, octant_ref, pack_ref, spread_ref):
    nb = owner_ref.shape[1]
    coarse = cell_ref.shape[1]
    whole, rest, height = spread_rows(coarse, nb)
    cell = cell_ref[...].astype(F32)
    owner = jnp.concatenate(
        [owner_ref[...].astype(F32), jnp.zeros((1, coarse - nb), F32)], axis=1
    )
    pack_ref[...] = jnp.concatenate([cell, owner], axis=0).astype(BF16)
    rows = [cell[k : k + 1, t * TILE : (t + 1) * TILE] for k in range(3) for t in range(whole)]
    tail = [cell[k : k + 1, whole * TILE :] for k in range(3)]
    tail.append(octant_ref[...].reshape(1, nb).astype(F32))
    tail.append(jnp.zeros((1, (height - 3 * whole) * TILE - 3 * rest - nb), F32))
    tail = jnp.concatenate(tail, axis=1)
    rows += [tail[:, t : t + TILE] for t in range(0, tail.shape[1], TILE)]
    rows = jnp.concatenate(rows, axis=0).astype(BF16)
    spread_ref[...] = jnp.broadcast_to(rows[None], spread_ref.shape)


def interleave_matrix(blk):
    group = TILE // blk
    point, lane = iota((TILE, TILE), 0), iota((TILE, TILE), 1)
    return ((point % blk == lane // group) & (point // blk == lane % group)).astype(BF16)


def source_columns(rows):
    forces = jnp.concatenate([rows[4:8], rows[4:8]], axis=0)
    places = jnp.concatenate([rows[0:4], rows[0:4]], axis=0)
    upper = iota(rows.shape, 0) < 4
    groups = []
    square = jnp.zeros_like(rows)
    inner = jnp.zeros_like(rows)
    for k in range(3):
        x_k = jnp.broadcast_to(rows[k : k + 1], rows.shape)
        product = x_k * forces
        high = product.astype(BF16).astype(F32)
        groups.append(jnp.where(upper, high, product - high))
        square = square + x_k * x_k
        inner = inner + x_k * rows[4 + k : 5 + k]
    rest = square * forces + inner * places
    high = rest.astype(BF16).astype(F32)
    middle = (rest - high).astype(BF16).astype(F32)
    groups.append(jnp.where(upper, high, middle))
    groups.append(jnp.where(upper, rest - high - middle, forces))
    return jnp.concatenate(groups, axis=0).astype(BF16)


def three_parts(x):
    high = x.astype(BF16).astype(F32)
    middle = (x - high).astype(BF16).astype(F32)
    return high, middle, x - high - middle


def distance_factors(rows, targets):
    def side(points, scale, extra, squares_first):
        square = jnp.sum(jnp.square(points[0:4]), axis=0, keepdims=True) + extra
        ones = [jnp.ones_like(square)] * 3
        squares = list(three_parts(square))
        parts = squares + ones if squares_first else ones + squares
        unused = jnp.zeros((7, points.shape[1]), F32)
        return jnp.concatenate([points[0:3] * scale] + parts + [unused], axis=0)

    source = side(rows, -2.0, 0.0, False).astype(BF16)
    target = side(targets, 1.0, EPSILON_SQ, True).T.astype(BF16)
    return source, target


def expanded_sums(rows, targets):
    columns = source_columns(rows)
    source, target = distance_factors(rows, targets)
    sums = None
    for start in range(0, rows.shape[1], SOURCE_TILES * TILE):
        part = slice(start, min(start + SOURCE_TILES * TILE, rows.shape[1]))
        inverse = lax.rsqrt(dot(target, source[:, part]))
        cubed = (inverse * inverse * inverse).astype(BF16)
        some = dot_lanes(columns[:, part], cubed)
        sums = some if sums is None else sums + some
    place = targets[0:4]
    moment = [sums[8 * k : 8 * k + 4] + sums[8 * k + 4 : 8 * k + 8] for k in range(3)]
    rest = sums[24:28] + sums[28:32] + sums[32:36]
    force = sums[36:40]
    square = jnp.sum(place * place, axis=0, keepdims=True)
    along = jnp.sum(place * force, axis=0, keepdims=True)
    trace = moment[0][0:1] + moment[1][1:2] + moment[2][2:3]
    cross = [jnp.sum(place * moment[k], axis=0, keepdims=True) for k in range(3)]
    cross = jnp.concatenate(cross + [jnp.zeros_like(trace)], axis=0)
    weighted = place[0:1] * moment[0] + place[1:2] * moment[1] + place[2:3] * moment[2]
    return (
        (square + 2.0 * EPSILON_SQ) * force + rest - 2.0 * weighted + place * (along - trace) - cross
    )


def direct_sums(rows, targets):
    strength = rows[4:8].astype(BF16)
    ones = jnp.ones((1, rows.shape[1]), F32)
    places = jnp.concatenate([rows[0:3], ones], axis=0).astype(BF16)
    upright = targets.T
    sums = None
    for start in range(0, rows.shape[1], TILE):
        stop = min(start + TILE, rows.shape[1])
        diffs = [upright[:, k : k + 1] - rows[k : k + 1, start:stop] for k in range(3)]
        dist = diffs[0] * diffs[0] + diffs[1] * diffs[1] + diffs[2] * diffs[2] + EPSILON_SQ
        inverse = lax.rsqrt(dist)
        cubed = inverse * inverse * inverse
        direct = ((dist + EPSILON_SQ) * cubed).astype(BF16)
        along = sum(diffs[k] * rows[4 + k : 5 + k, start:stop] for k in range(3))
        radial = (along * cubed).astype(BF16)
        near = dot_lanes(strength[:, start:stop], direct)
        away = dot_lanes(places[:, start:stop], radial)
        part = jnp.concatenate([near, away], axis=0)
        sums = part if sums is None else sums + part
    return sums[0:4] + targets[0:4] * sums[7:8] - sums[4:8]


def near_kernel(blk, packs_given, *refs):
    cell_ref, owner_ref, *pack_refs = refs[: packs_given + 2]
    bend_ref, _, up_hbm, out_ref, up_ref, *refs = refs[packs_given + 2 :]
    places_ref, bent_ref, sort_ref, part_ref, rows_ref, found_ref, sems = refs
    chunks = lane_chunks(up_ref.shape[1], COPY_TILES)
    copies = [
        pltpu.make_async_copy(up_hbm.at[:, a:b], up_ref.at[:, a:b], sems.at[n])
        for n, (a, b) in enumerate(chunks)
    ]
    for copy in copies:
        copy.start()
    cells = packs_given + 1
    fine = up_ref.shape[1]
    nb = fine // blk
    capacity = nb // cells + 2
    spots = cells * capacity
    group = TILE // blk
    tiles = -(-fine // TILE)

    def prepare():
        packs = [ref[...].astype(F32) for ref in pack_refs]
        none = jnp.zeros((1, cell_ref.shape[1]), F32)
        coarse = [jnp.concatenate([cell_ref[...].astype(F32), none], axis=0)]
        coarse += [jnp.where(iota(pack.shape, 0) < 3, pack, 0.0) for pack in packs]
        owners = [owner_ref[...].astype(F32)] + [pack[3:4, 0:nb] for pack in packs]
        point_rows, force_rows = [], []
        for three in coarse:
            point_rows += [three, jnp.zeros_like(three)]
            force_rows += [jnp.zeros_like(three), three]
        places_ref[...] = jnp.concatenate(point_rows, axis=0).astype(BF16)
        force_rows = jnp.concatenate(force_rows, axis=0).astype(BF16)
        bent_ref[...] = dot(force_rows, bend_ref[...]).astype(BF16)
        leaf_ids = iota((cells, nb), 0).astype(F32)
        chosen = jnp.concatenate([(leaf_ids == own).astype(F32) for own in owners], axis=0)
        earlier = (iota((nb, nb), 0) < iota((nb, nb), 1)).astype(BF16)
        before = dot(chosen.astype(BF16), earlier) * chosen
        spot_ids = iota((spots, nb), 0).astype(F32)
        for c in range(cells):
            rank = jnp.sum(before[c * cells : (c + 1) * cells], axis=0, keepdims=True)
            sort_ref[c] = (spot_ids == owners[c] * capacity + rank).astype(BF16)

    def part_points(n):
        a, b = chunks[n]
        copies[n].wait()
        fields = bent_ref[:, a:b] + dot(places_ref[...], up_ref[:, a:b]).astype(BF16)
        if (b - a) % TILE:
            rest = jnp.zeros((8 * cells, -(b - a) % TILE), BF16)
            fields = jnp.concatenate([fields, rest], axis=1)
        stacked = [fields[:, t : t + TILE] for t in range(0, fields.shape[1], TILE)]
        parted = dot(jnp.concatenate(stacked, axis=0), interleave_matrix(blk))
        first = a // TILE * 8 * cells
        part_ref[first : first + parted.shape[0]] = parted

    def finish():
        near_sums(blk, cells, fine, out_ref, sort_ref, part_ref, rows_ref, found_ref)

    in_stages(
        prepare, *[functools.partial(part_points, n) for n in range(len(chunks))], finish
    )


def near_sums(blk, cells, fine, out_ref, sort_ref, part_ref, rows_ref, found_ref):
    nb = fine // blk
    capacity = nb // cells + 2
    group = TILE // blk
    tiles = -(-fine // TILE)
    mix = interleave_matrix(blk)
    parted = part_ref[...]
    sorts = [sort_ref[c] for c in range(cells)]
    by_point = [
        jnp.concatenate(
            [
                parted[t * 8 * cells : (t + 1) * 8 * cells, k * group : (k + 1) * group]
                for t in range(tiles)
            ],
            axis=1,
        )[:, 0:nb]
        for k in range(blk)
    ]
    by_leaf = []
    for c in range(cells):
        rows = jnp.concatenate([by_point[k][8 * c : 8 * c + 8] for k in range(blk)], axis=0)
        by_leaf.append(dot_lanes(rows.astype(BF16), sorts[c]))
    for leaf in range(cells):
        rows_ref[leaf] = jnp.concatenate(
            [
                by_leaf[c][8 * k : 8 * k + 8, leaf * capacity : (leaf + 1) * capacity]
                for c in range(cells)
                for k in range(blk)
            ],
            axis=1,
        )
    farthest = jnp.max(
        sum(jnp.square(by_leaf[c][8 * k : 8 * k + 4]) for c in range(cells) for k in range(blk))
    )

    def each_leaf(sums, leaf, _):
        rows = rows_ref[leaf]
        velocity = sums(rows, rows[:, 0 : capacity * blk]) * STOKES_SCALE
        found_ref[leaf] = jnp.concatenate(
            [velocity[:, k * capacity : (k + 1) * capacity] for k in range(blk)], axis=0
        )
        return 0

    lax.fori_loop(0, cells, functools.partial(each_leaf, expanded_sums), 0, unroll=cells <= 4)

    @pl.when(farthest > EXPAND_LIMIT)
    def _():
        lax.fori_loop(0, cells, functools.partial(each_leaf, direct_sums), 0)

    found = jnp.concatenate([found_ref[leaf] for leaf in range(cells)], axis=1)
    high, low = split_bf16(found)
    back = dot(jnp.concatenate([high, low], axis=0), sorts[0])
    back = back[: 4 * blk] + back[4 * blk :]
    back = jnp.concatenate([back, jnp.zeros((4 * blk, tiles * group - nb), F32)], axis=1)
    pieces = [
        jnp.concatenate(
            [back[4 * k : 4 * k + 4, t * group : (t + 1) * group] for k in range(blk)], axis=1
        )
        for t in range(tiles)
    ]
    high, low = split_bf16(jnp.concatenate(pieces, axis=0))
    natural = dot_lanes(high, mix) + dot_lanes(low, mix)
    for t in range(tiles):
        stop = min((t + 1) * TILE, fine)
        out_ref[0:4, t * TILE : stop] = natural[4 * t : 4 * t + 4, 0 : stop - t * TILE]

def far_kernel(blk, cells, regions, *refs):
    list_ref, packs_ref, near_ref, bend_ref, dens_ref, *in_hbm = refs[:8]
    out_ref, trans_ref, eval_ref, smooth_ref, density_ref, total_ref, sems = refs[8:]
    trans_copy, eval_copy, smooth_copy = [
        pltpu.make_async_copy(src, dst, sems.at[n])
        for n, (src, dst) in enumerate(zip(in_hbm, (trans_ref, eval_ref, smooth_ref)))
    ]
    for copy in (trans_copy, eval_copy, smooth_copy):
        copy.start()
    listed = list_ref.shape[1]
    fine = bend_ref.shape[1]
    nb = fine // blk
    points = eval_ref.shape[0]
    per_region = OCTANTS_PER_OWNER * cells
    rows = cells * 3 * listed
    devices = cells * regions
    span = 3 * listed
    whole, rest, height = spread_rows(bend_ref.shape[0], nb)

    def densities():
        row = iota((rows, 1), 0)
        entry, comp, cell = row % listed, row // listed % 3, row // span
        octant = jnp.zeros((rows, 1), jnp.int32)
        region = jnp.zeros((rows, 1), jnp.int32)
        for l in range(listed):
            wanted = list_ref[0:1, l : l + 1]
            octant = jnp.where(entry == l, wanted % per_region, octant)
            region = jnp.where(entry == l, wanted // per_region, region)
        source = (cell * regions + region) * height
        columns = iota((rows, devices * height), 1)
        flat = packs_ref[...].reshape(devices * height, TILE)

        def take(n):
            return dot((columns == source + n).astype(BF16), flat)

        coarse = [take(comp * whole + t) for t in range(whole)]
        tail = jnp.concatenate([take(n) for n in range(3 * whole, height)], axis=1)
        left = [tail[:, k * rest : (k + 1) * rest] for k in range(3)]
        coarse.append(jnp.where(comp == 0, left[0], jnp.where(comp == 1, left[1], left[2])))
        coarse = jnp.concatenate(coarse, axis=1)
        marks = tail[:, 3 * rest : 3 * rest + nb]
        inside = (marks == octant.astype(F32)).astype(BF16)
        widen = (iota((nb, fine), 0) == iota((nb, fine), 1) // blk).astype(BF16)
        inside = dot(inside, widen)
        forces = dot(coarse.astype(BF16), bend_ref[...]).astype(BF16).astype(F32)
        density = dot_lanes((forces * inside).astype(BF16), dens_ref[...])
        density_ref[...] = sum(density[c * span : (c + 1) * span] for c in range(cells))

    def totals():
        trans_copy.wait()
        eval_copy.wait()
        density = density_ref[...].astype(BF16)
        expansion = sum(
            dot(density[k * listed : (k + 1) * listed], trans_ref[k * points : (k + 1) * points, :])
            for k in range(3)
        )
        far = jnp.sum(expansion.astype(BF16).astype(F32), axis=0, keepdims=True)
        far = jnp.concatenate(
            [far[:, k * points : (k + 1) * points] for k in range(3)]
            + [jnp.zeros((1, points), F32)],
            axis=0,
        )
        total_ref[...] = near_ref[0:4, :] + dot(far.astype(BF16), eval_ref[...])

    def velocities():
        smooth_copy.wait()
        velocity = dot_lanes(total_ref[...].astype(BF16), smooth_ref[...])
        for k in range(3):
            out_ref[k] = velocity[k : k + 1]

    in_stages(densities, totals, velocities)


def in_place(x):
    return pltpu.with_memory_space_constraint(x, pltpu.HBM)


def vmem(megabytes):
    return pltpu.CompilerParams(vmem_limit_bytes=megabytes << 20)


def on_device(
    cell_shape,
    upsample,
    bending,
    to_density,
    translate,
    evaluate,
    smoothing,
    block_owner,
    block_octant,
    far_list,
):
    cells, regions = lax.axis_size("cells"), lax.axis_size("region")
    coarse, fine = upsample.shape
    nb = block_owner.shape[0]
    blk = fine // nb
    own_cell, own_blocks = cell_shape.reshape(3, coarse), block_owner.reshape(1, nb)
    pack, spread = pl.pallas_call(
        pack_kernel,
        out_shape=(
            jax.ShapeDtypeStruct((4, coarse), BF16),
            jax.ShapeDtypeStruct((cells * regions, spread_rows(coarse, nb)[2], TILE), BF16),
        ),
        cost_estimate=pl.CostEstimate(flops=5 * 10**10, bytes_accessed=10**6, transcendentals=0),
        name="pack",
    )(own_cell, own_blocks, block_octant)
    others = [
        lax.ppermute(pack, "cells", [(i, i ^ k) for i in range(cells)])
        for k in sorted(range(1, cells), reverse=True)
    ]
    everyone = lax.all_to_all(spread, ("cells", "region"), split_axis=0, concat_axis=0, tiled=True)
    in_vmem = pl.BlockSpec(memory_space=pltpu.VMEM)
    in_hbm = pl.BlockSpec(memory_space=pltpu.HBM)
    points = cells * (nb // cells + 2) * blk
    near = pl.pallas_call(
        functools.partial(near_kernel, blk, len(others)),
        out_shape=jax.ShapeDtypeStruct((4, fine), F32),
        in_specs=[in_vmem] * (cells + 3) + [in_hbm],
        scratch_shapes=[
            pltpu.VMEM(upsample.shape, BF16),
            pltpu.VMEM((8 * cells, coarse), BF16),
            pltpu.VMEM((8 * cells, fine), BF16),
            pltpu.VMEM((cells, points // blk, nb), BF16),
            pltpu.VMEM((-(-fine // TILE) * 8 * cells, TILE), F32),
            pltpu.VMEM((cells, 8, points), F32),
            pltpu.VMEM((cells, 4 * blk, points // (cells * blk)), F32),
            pltpu.SemaphoreType.DMA((len(lane_chunks(fine, COPY_TILES)),)),
        ],
        compiler_params=vmem(40),
        cost_estimate=pl.CostEstimate(flops=5 * 10**10, bytes_accessed=10**6, transcendentals=0),
        name="near",
    )(own_cell, own_blocks, *others, bending, to_density.T, in_place(upsample))
    later = [in_place(x) for x in (translate, evaluate, smoothing.T)]
    velocity = pl.pallas_call(
        functools.partial(far_kernel, blk, cells, regions),
        out_shape=jax.ShapeDtypeStruct((3, 1, coarse), F32),
        in_specs=[in_vmem] * 5 + [in_hbm] * 3,
        scratch_shapes=[pltpu.VMEM(x.shape, BF16) for x in later]
        + [
            pltpu.VMEM((3 * far_list.shape[1], evaluate.shape[0]), F32),
            pltpu.VMEM((4, fine), F32),
            pltpu.SemaphoreType.DMA((3,)),
        ],
        compiler_params=vmem(32),
        name="far",
    )(far_list, everyone, near, bending, to_density.T, *later)
    return velocity.transpose(1, 0, 2)


def solution(mesh):
    own = P(("cells", "region"))
    return jax.shard_map(
        on_device,
        mesh=mesh,
        in_specs=(own, P(), P(), P(), P(), P(), P(), own, own, own),
        out_specs=own,
        check_vma=False,
    )
```

```python
import functools

import jax
import jax.numpy as jnp
from jax import lax
from jax.experimental import pallas as pl
from jax.experimental.pallas import tpu as pltpu
from jax.sharding import PartitionSpec as P

EPSILON_SQ = 0.0625
STOKES_SCALE = 1.0 / (8.0 * 3.141592653589793)
EXPAND_LIMIT = 128.0
TILE = 256
OCTANTS_PER_OWNER = 2
COPY_TILES = 3
SOURCE_TILES = 5
F32 = jnp.float32
BF16 = jnp.bfloat16
LANES = (((1,), (1,)), ((), ()))


def iota(shape, dim):
    return lax.broadcasted_iota(jnp.int32, shape, dim)


def dot(a, b):
    return jnp.dot(a, b, preferred_element_type=F32)


def dot_lanes(a, b):
    return lax.dot_general(a, b, LANES, preferred_element_type=F32)


def split_bf16(x):
    high = x.astype(BF16)
    return high, (x - high.astype(F32)).astype(BF16)


def lane_chunks(lanes, tiles):
    return [(start, min(start + tiles * TILE, lanes)) for start in range(0, lanes, tiles * TILE)]


def in_stages(*stages):
    def step(at, _):
        for n, stage in enumerate(stages):
            pl.when(at == n)(stage)
        return 0

    lax.fori_loop(0, len(stages), step, 0)


def spread_rows(coarse, nb):
    whole, rest = coarse // TILE, coarse % TILE
    return whole, rest, 3 * whole + -(-(3 * rest + nb) // TILE)


def pack_kernel(cell_ref, owner_ref, octant_ref, pack_ref, spread_ref):
    nb = owner_ref.shape[1]
    coarse = cell_ref.shape[1]
    whole, rest, height = spread_rows(coarse, nb)
    cell = cell_ref[...].astype(F32)
    owner = jnp.concatenate(
        [owner_ref[...].astype(F32), jnp.zeros((1, coarse - nb), F32)], axis=1
    )
    pack_ref[...] = jnp.concatenate([cell, owner], axis=0).astype(BF16)
    rows = [cell[k : k + 1, t * TILE : (t + 1) * TILE] for k in range(3) for t in range(whole)]
    tail = [cell[k : k + 1, whole * TILE :] for k in range(3)]
    tail.append(octant_ref[...].reshape(1, nb).astype(F32))
    tail.append(jnp.zeros((1, (height - 3 * whole) * TILE - 3 * rest - nb), F32))
    tail = jnp.concatenate(tail, axis=1)
    rows += [tail[:, t : t + TILE] for t in range(0, tail.shape[1], TILE)]
    rows = jnp.concatenate(rows, axis=0).astype(BF16)
    spread_ref[...] = jnp.broadcast_to(rows[None], spread_ref.shape)


def interleave_matrix(blk):
    group = TILE // blk
    point, lane = iota((TILE, TILE), 0), iota((TILE, TILE), 1)
    return ((point % blk == lane // group) & (point // blk == lane % group)).astype(BF16)


def source_columns(rows):
    forces = jnp.concatenate([rows[4:8], rows[4:8]], axis=0)
    places = jnp.concatenate([rows[0:4], rows[0:4]], axis=0)
    upper = iota(rows.shape, 0) < 4
    groups = []
    square = jnp.zeros_like(rows)
    inner = jnp.zeros_like(rows)
    for k in range(3):
        x_k = jnp.broadcast_to(rows[k : k + 1], rows.shape)
        product = x_k * forces
        high = product.astype(BF16).astype(F32)
        groups.append(jnp.where(upper, high, product - high))
        square = square + x_k * x_k
        inner = inner + x_k * rows[4 + k : 5 + k]
    rest = square * forces + inner * places
    high = rest.astype(BF16).astype(F32)
    middle = (rest - high).astype(BF16).astype(F32)
    groups.append(jnp.where(upper, high, middle))
    groups.append(jnp.where(upper, rest - high - middle, forces))
    return jnp.concatenate(groups, axis=0).astype(BF16)


def three_parts(x):
    high = x.astype(BF16).astype(F32)
    middle = (x - high).astype(BF16).astype(F32)
    return high, middle, x - high - middle


def distance_factors(rows, targets):
    def side(points, scale, extra, squares_first):
        square = jnp.sum(jnp.square(points[0:4]), axis=0, keepdims=True) + extra
        ones = [jnp.ones_like(square)] * 3
        squares = list(three_parts(square))
        parts = squares + ones if squares_first else ones + squares
        unused = jnp.zeros((7, points.shape[1]), F32)
        return jnp.concatenate([points[0:3] * scale] + parts + [unused], axis=0)

    source = side(rows, -2.0, 0.0, False).astype(BF16)
    target = side(targets, 1.0, EPSILON_SQ, True).T.astype(BF16)
    return source, target


def expanded_sums(rows, targets):
    columns = source_columns(rows)
    source, target = distance_factors(rows, targets)
    sums = None
    for start in range(0, rows.shape[1], SOURCE_TILES * TILE):
        part = slice(start, min(start + SOURCE_TILES * TILE, rows.shape[1]))
        inverse = lax.rsqrt(dot(target, source[:, part]))
        cubed = (inverse * inverse * inverse).astype(BF16)
        some = dot_lanes(columns[:, part], cubed)
        sums = some if sums is None else sums + some
    place = targets[0:4]
    moment = [sums[8 * k : 8 * k + 4] + sums[8 * k + 4 : 8 * k + 8] for k in range(3)]
    rest = sums[24:28] + sums[28:32] + sums[32:36]
    force = sums[36:40]
    square = jnp.sum(place * place, axis=0, keepdims=True)
    along = jnp.sum(place * force, axis=0, keepdims=True)
    trace = moment[0][0:1] + moment[1][1:2] + moment[2][2:3]
    cross = [jnp.sum(place * moment[k], axis=0, keepdims=True) for k in range(3)]
    cross = jnp.concatenate(cross + [jnp.zeros_like(trace)], axis=0)
    weighted = place[0:1] * moment[0] + place[1:2] * moment[1] + place[2:3] * moment[2]
    return (
        (square + 2.0 * EPSILON_SQ) * force + rest - 2.0 * weighted + place * (along - trace) - cross
    )


def direct_sums(rows, targets):
    strength = rows[4:8].astype(BF16)
    ones = jnp.ones((1, rows.shape[1]), F32)
    places = jnp.concatenate([rows[0:3], ones], axis=0).astype(BF16)
    upright = targets.T
    sums = None
    for start in range(0, rows.shape[1], TILE):
        stop = min(start + TILE, rows.shape[1])
        diffs = [upright[:, k : k + 1] - rows[k : k + 1, start:stop] for k in range(3)]
        dist = diffs[0] * diffs[0] + diffs[1] * diffs[1] + diffs[2] * diffs[2] + EPSILON_SQ
        inverse = lax.rsqrt(dist)
        cubed = inverse * inverse * inverse
        direct = ((dist + EPSILON_SQ) * cubed).astype(BF16)
        along = sum(diffs[k] * rows[4 + k : 5 + k, start:stop] for k in range(3))
        radial = (along * cubed).astype(BF16)
        near = dot_lanes(strength[:, start:stop], direct)
        away = dot_lanes(places[:, start:stop], radial)
        part = jnp.concatenate([near, away], axis=0)
        sums = part if sums is None else sums + part
    return sums[0:4] + targets[0:4] * sums[7:8] - sums[4:8]


def near_kernel(blk, packs_given, *refs):
    cell_ref, owner_ref, *pack_refs = refs[: packs_given + 2]
    bend_ref, _, up_hbm, out_ref, up_ref, *refs = refs[packs_given + 2 :]
    places_ref, bent_ref, sort_ref, part_ref, rows_ref, found_ref, sems = refs
    chunks = lane_chunks(up_ref.shape[1], COPY_TILES)
    copies = [
        pltpu.make_async_copy(up_hbm.at[:, a:b], up_ref.at[:, a:b], sems.at[n])
        for n, (a, b) in enumerate(chunks)
    ]
    for copy in copies:
        copy.start()
    cells = packs_given + 1
    fine = up_ref.shape[1]
    nb = fine // blk
    capacity = nb // cells + 2
    spots = cells * capacity
    group = TILE // blk
    tiles = -(-fine // TILE)

    def prepare():
        packs = [ref[...].astype(F32) for ref in pack_refs]
        none = jnp.zeros((1, cell_ref.shape[1]), F32)
        coarse = [jnp.concatenate([cell_ref[...].astype(F32), none], axis=0)]
        coarse += [jnp.where(iota(pack.shape, 0) < 3, pack, 0.0) for pack in packs]
        owners = [owner_ref[...].astype(F32)] + [pack[3:4, 0:nb] for pack in packs]
        point_rows, force_rows = [], []
        for three in coarse:
            point_rows += [three, jnp.zeros_like(three)]
            force_rows += [jnp.zeros_like(three), three]
        places_ref[...] = jnp.concatenate(point_rows, axis=0).astype(BF16)
        force_rows = jnp.concatenate(force_rows, axis=0).astype(BF16)
        bent_ref[...] = dot(force_rows, bend_ref[...]).astype(BF16)
        leaf_ids = iota((cells, nb), 0).astype(F32)
        chosen = jnp.concatenate([(leaf_ids == own).astype(F32) for own in owners], axis=0)
        earlier = (iota((nb, nb), 0) < iota((nb, nb), 1)).astype(BF16)
        before = dot(chosen.astype(BF16), earlier) * chosen
        spot_ids = iota((spots, nb), 0).astype(F32)
        for c in range(cells):
            rank = jnp.sum(before[c * cells : (c + 1) * cells], axis=0, keepdims=True)
            sort_ref[c] = (spot_ids == owners[c] * capacity + rank).astype(BF16)

    def part_points(n):
        a, b = chunks[n]
        copies[n].wait()
        fields = bent_ref[:, a:b] + dot(places_ref[...], up_ref[:, a:b]).astype(BF16)
        if (b - a) % TILE:
            rest = jnp.zeros((8 * cells, -(b - a) % TILE), BF16)
            fields = jnp.concatenate([fields, rest], axis=1)
        stacked = [fields[:, t : t + TILE] for t in range(0, fields.shape[1], TILE)]
        parted = dot(jnp.concatenate(stacked, axis=0), interleave_matrix(blk))
        first = a // TILE * 8 * cells
        part_ref[first : first + parted.shape[0]] = parted

    def finish():
        near_sums(blk, cells, fine, out_ref, sort_ref, part_ref, rows_ref, found_ref)

    in_stages(
        prepare, *[functools.partial(part_points, n) for n in range(len(chunks))], finish
    )


def near_sums(blk, cells, fine, out_ref, sort_ref, part_ref, rows_ref, found_ref):
    nb = fine // blk
    capacity = nb // cells + 2
    group = TILE // blk
    tiles = -(-fine // TILE)
    mix = interleave_matrix(blk)
    parted = part_ref[...]
    sorts = [sort_ref[c] for c in range(cells)]
    by_point = [
        jnp.concatenate(
            [
                parted[t * 8 * cells : (t + 1) * 8 * cells, k * group : (k + 1) * group]
                for t in range(tiles)
            ],
            axis=1,
        )[:, 0:nb]
        for k in range(blk)
    ]
    by_leaf = []
    for c in range(cells):
        rows = jnp.concatenate([by_point[k][8 * c : 8 * c + 8] for k in range(blk)], axis=0)
        by_leaf.append(dot_lanes(rows.astype(BF16), sorts[c]))
    for leaf in range(cells):
        rows_ref[leaf] = jnp.concatenate(
            [
                by_leaf[c][8 * k : 8 * k + 8, leaf * capacity : (leaf + 1) * capacity]
                for c in range(cells)
                for k in range(blk)
            ],
            axis=1,
        )
    farthest = jnp.max(
        sum(jnp.square(by_leaf[c][8 * k : 8 * k + 4]) for c in range(cells) for k in range(blk))
    )

    def each_leaf(sums, leaf, _):
        rows = rows_ref[leaf]
        velocity = sums(rows, rows[:, 0 : capacity * blk]) * STOKES_SCALE
        found_ref[leaf] = jnp.concatenate(
            [velocity[:, k * capacity : (k + 1) * capacity] for k in range(blk)], axis=0
        )
        return 0

    lax.fori_loop(0, cells, functools.partial(each_leaf, expanded_sums), 0, unroll=cells <= 4)

    @pl.when(farthest > EXPAND_LIMIT)
    def _():
        lax.fori_loop(0, cells, functools.partial(each_leaf, direct_sums), 0)

    found = jnp.concatenate([found_ref[leaf] for leaf in range(cells)], axis=1)
    high, low = split_bf16(found)
    back = dot(jnp.concatenate([high, low], axis=0), sorts[0])
    back = back[: 4 * blk] + back[4 * blk :]
    back = jnp.concatenate([back, jnp.zeros((4 * blk, tiles * group - nb), F32)], axis=1)
    pieces = [
        jnp.concatenate(
            [back[4 * k : 4 * k + 4, t * group : (t + 1) * group] for k in range(blk)], axis=1
        )
        for t in range(tiles)
    ]
    high, low = split_bf16(jnp.concatenate(pieces, axis=0))
    natural = dot_lanes(high, mix) + dot_lanes(low, mix)
    for t in range(tiles):
        stop = min((t + 1) * TILE, fine)
        out_ref[0:4, t * TILE : stop] = natural[4 * t : 4 * t + 4, 0 : stop - t * TILE]

def far_kernel(blk, cells, regions, *refs):
    list_ref, packs_ref, near_ref, bend_ref, dens_ref, *in_hbm = refs[:8]
    out_ref, trans_ref, eval_ref, smooth_ref, density_ref, sems = refs[8:]
    trans_copy, eval_copy, smooth_copy = [
        pltpu.make_async_copy(src, dst, sems.at[n])
        for n, (src, dst) in enumerate(zip(in_hbm, (trans_ref, eval_ref, smooth_ref)))
    ]
    for copy in (trans_copy, eval_copy, smooth_copy):
        copy.start()
    listed = list_ref.shape[1]
    fine = bend_ref.shape[1]
    nb = fine // blk
    points = eval_ref.shape[0]
    per_region = OCTANTS_PER_OWNER * cells
    rows = cells * 3 * listed
    devices = cells * regions
    span = 3 * listed
    whole, rest, height = spread_rows(bend_ref.shape[0], nb)

    def densities():
        row = iota((rows, 1), 0)
        entry, comp, cell = row % listed, row // listed % 3, row // span
        octant = jnp.zeros((rows, 1), jnp.int32)
        region = jnp.zeros((rows, 1), jnp.int32)
        for l in range(listed):
            wanted = list_ref[0:1, l : l + 1]
            octant = jnp.where(entry == l, wanted % per_region, octant)
            region = jnp.where(entry == l, wanted // per_region, region)
        source = (cell * regions + region) * height
        columns = iota((rows, devices * height), 1)
        flat = packs_ref[...].reshape(devices * height, TILE)

        def take(n):
            return dot((columns == source + n).astype(BF16), flat)

        coarse = [take(comp * whole + t) for t in range(whole)]
        tail = jnp.concatenate([take(n) for n in range(3 * whole, height)], axis=1)
        left = [tail[:, k * rest : (k + 1) * rest] for k in range(3)]
        coarse.append(jnp.where(comp == 0, left[0], jnp.where(comp == 1, left[1], left[2])))
        coarse = jnp.concatenate(coarse, axis=1)
        marks = tail[:, 3 * rest : 3 * rest + nb]
        inside = (marks == octant.astype(F32)).astype(BF16)
        widen = (iota((nb, fine), 0) == iota((nb, fine), 1) // blk).astype(BF16)
        inside = dot(inside, widen)
        forces = dot(coarse.astype(BF16), bend_ref[...]).astype(BF16).astype(F32)
        density = dot_lanes((forces * inside).astype(BF16), dens_ref[...])
        density_ref[...] = sum(density[c * span : (c + 1) * span] for c in range(cells))

    def velocities():
        trans_copy.wait()
        eval_copy.wait()
        density = density_ref[...].astype(BF16)
        expansion = sum(
            dot(density[k * listed : (k + 1) * listed], trans_ref[k * points : (k + 1) * points, :])
            for k in range(3)
        )
        far = jnp.sum(expansion.astype(BF16).astype(F32), axis=0, keepdims=True)
        far = jnp.concatenate(
            [far[:, k * points : (k + 1) * points] for k in range(3)]
            + [jnp.zeros((1, points), F32)],
            axis=0,
        )
        total = near_ref[0:4, :] + dot(far.astype(BF16), eval_ref[...])
        smooth_copy.wait()
        velocity = dot_lanes(total.astype(BF16), smooth_ref[...])
        for k in range(3):
            out_ref[k] = velocity[k : k + 1]

    in_stages(densities, velocities)


def in_place(x):
    return pltpu.with_memory_space_constraint(x, pltpu.HBM)


def vmem(megabytes):
    return pltpu.CompilerParams(vmem_limit_bytes=megabytes << 20)


def on_device(
    cell_shape,
    upsample,
    bending,
    to_density,
    translate,
    evaluate,
    smoothing,
    block_owner,
    block_octant,
    far_list,
):
    cells, regions = lax.axis_size("cells"), lax.axis_size("region")
    coarse, fine = upsample.shape
    nb = block_owner.shape[0]
    blk = fine // nb
    own_cell, own_blocks = cell_shape.reshape(3, coarse), block_owner.reshape(1, nb)
    pack, spread = pl.pallas_call(
        pack_kernel,
        out_shape=(
            jax.ShapeDtypeStruct((4, coarse), BF16),
            jax.ShapeDtypeStruct((cells * regions, spread_rows(coarse, nb)[2], TILE), BF16),
        ),
        cost_estimate=pl.CostEstimate(flops=5 * 10**10, bytes_accessed=10**6, transcendentals=0),
        name="pack",
    )(own_cell, own_blocks, block_octant)
    others = [
        lax.ppermute(pack, "cells", [(i, i ^ k) for i in range(cells)])
        for k in sorted(range(1, cells), reverse=True)
    ]
    everyone = lax.all_to_all(spread, ("cells", "region"), split_axis=0, concat_axis=0, tiled=True)
    in_vmem = pl.BlockSpec(memory_space=pltpu.VMEM)
    in_hbm = pl.BlockSpec(memory_space=pltpu.HBM)
    points = cells * (nb // cells + 2) * blk
    near = pl.pallas_call(
        functools.partial(near_kernel, blk, len(others)),
        out_shape=jax.ShapeDtypeStruct((4, fine), F32),
        in_specs=[in_vmem] * (cells + 3) + [in_hbm],
        scratch_shapes=[
            pltpu.VMEM(upsample.shape, BF16),
            pltpu.VMEM((8 * cells, coarse), BF16),
            pltpu.VMEM((8 * cells, fine), BF16),
            pltpu.VMEM((cells, points // blk, nb), BF16),
            pltpu.VMEM((-(-fine // TILE) * 8 * cells, TILE), F32),
            pltpu.VMEM((cells, 8, points), F32),
            pltpu.VMEM((cells, 4 * blk, points // (cells * blk)), F32),
            pltpu.SemaphoreType.DMA((len(lane_chunks(fine, COPY_TILES)),)),
        ],
        compiler_params=vmem(40),
        cost_estimate=pl.CostEstimate(flops=5 * 10**10, bytes_accessed=10**6, transcendentals=0),
        name="near",
    )(own_cell, own_blocks, *others, bending, to_density.T, in_place(upsample))
    later = [in_place(x) for x in (translate, evaluate, smoothing.T)]
    velocity = pl.pallas_call(
        functools.partial(far_kernel, blk, cells, regions),
        out_shape=jax.ShapeDtypeStruct((3, 1, coarse), F32),
        in_specs=[in_vmem] * 5 + [in_hbm] * 3,
        scratch_shapes=[pltpu.VMEM(x.shape, BF16) for x in later]
        + [
            pltpu.VMEM((3 * far_list.shape[1], evaluate.shape[0]), F32),
            pltpu.SemaphoreType.DMA((3,)),
        ],
        compiler_params=vmem(32),
        name="far",
    )(far_list, everyone, near, bending, to_density.T, *later)
    return velocity.transpose(1, 0, 2)


def solution(mesh):
    own = P(("cells", "region"))
    return jax.shard_map(
        on_device,
        mesh=mesh,
        in_specs=(own, P(), P(), P(), P(), P(), P(), own, own, own),
        out_specs=own,
        check_vma=False,
    )
```
